512 devices in a mesh: section: 8 (over x, core), mp: 64 (over y, z).
Axes of the slice: x: 4, y: 4, z: 16, core: 2. Of those that a mesh axis runs over, the one named last changes fastest.
Arguments:
- section_in: bfloat16 [8, 128, 8192], P('section', 'mp'), may hold values from -8 to 8
- fresh: bfloat16 [128, 8192], P('mp'), may hold values from -8 to 8
- latents: bfloat16 [72, 64, 1280], P(None, 'mp'), may hold values from -4 to 4
- image_order: int32 [72], replicated, may hold values from 0 to 71, each once
- token_mask: int32 [9, 128, 8], replicated, may hold values from 0 to 1, as said below
- norm_gain: bfloat16 [8, 8192], P('section'), may hold values from 0.5 to 1.5
- wq: bfloat16 [8, 8192, 8192], P('section', None, 'mp'), may hold values from -0.1875 to 0.1875
- wkv: bfloat16 [8, 2, 1280, 8192], P('section', None, None, 'mp'), may hold values from -3 to 3
- wo: bfloat16 [8, 8192, 8192], P('section', None, 'mp'), may hold values from -0.1875 to 0.1875
- alpha: float32 [8, 8192], P('section', 'mp'), may hold values from 0.5 to 1.5
Outputs:
- first_out: bfloat16 [8, 128, 8192], P('section', 'mp')
- second_out: bfloat16 [8, 128, 8192], P('section', 'mp')
The draws below stay inside these ranges and needn't reach their ends.
Inputs may be any that keep to these rules, and one draw needn't show every extreme that they name: `image_order`: each image index once. `token_mask`: in every micro-batch the first 8 tokens, and possibly more, see no slot.
All inputs are finite; a program needn't handle non-finite values.
Results may differ from the reference program's by a relative error of at most 0.012.
The reference program's roundings to bfloat16 on the way (of `normed`, `queries`, `picked`, `probs`, `attended` and `branch`) count: a program that leaves them out, or rounds other values in their place, can miss the bound.
Values may be sent and summed in bfloat16 or wider, within the bound.
A program may use at most 64 MiB of HBM per device.

```python
import math
import jax
import jax.numpy as jnp
from jax import lax

D = 8192
HEADS = 64
HD = 128
VD = 1280
LAT = 64
MB = 128
IMG_MB = 8
MICRO = 9
IMAGES = 72
N_SECTION = 8


def column_profile(key):
    position = jnp.arange(D, dtype=jnp.float32) / D
    jitter = jnp.exp(jax.random.uniform(key, (D,), jnp.float32, math.log(0.6), math.log(1.6)))
    return jnp.exp(math.log(3.0) * (position - 0.5)) * jitter


def draw_section_in(key, part):
    key = jax.random.fold_in(key, 1)
    noise_key, column_key = jax.random.split(key, 2)
    shape = (N_SECTION, MB, D)
    profile = column_profile(column_key)
    noise = jax.random.normal(noise_key, shape, jnp.float32)
    return jnp.clip(noise * profile[None, None, :], -8.0, 8.0).astype(jnp.bfloat16)


def draw_fresh(key, part):
    key = jax.random.fold_in(key, 2)
    noise_key, column_key = jax.random.split(key, 2)
    shape = (MB, D)
    profile = column_profile(column_key)
    noise = jax.random.normal(noise_key, shape, jnp.float32)
    return jnp.clip(noise * profile[None, :], -8.0, 8.0).astype(jnp.bfloat16)


def draw_latents(key, part):
    key = jax.random.fold_in(key, 3)
    shape = (IMAGES, LAT, VD)
    result = jnp.clip(jax.random.normal(key, shape, jnp.float32), -4.0, 4.0)
    return result.astype(jnp.bfloat16)


def draw_wkv(key, part):
    key = jax.random.fold_in(key, 5)
    base_key = jax.random.fold_in(key, 0)
    base = jax.random.normal(base_key, (N_SECTION, 2, VD, D), jnp.float32) * VD ** (-0.5)
    base = jnp.clip(base, -6.0 * VD ** (-0.5), 6.0 * VD ** (-0.5))
    return base.astype(jnp.bfloat16)


def draw_token_mask(key, part):
    key = jax.random.fold_in(key, 7)
    coin_key, lead_key = jax.random.split(key)
    coin_bits = jax.random.randint(coin_key, (MICRO, MB, IMG_MB), 0, 2)
    lead_count = jax.random.randint(lead_key, (MICRO, 1, 1), MB // 16, MB // 4 + 1)
    position = jnp.arange(MB)[None, :, None]
    return jnp.where(position >= lead_count, coin_bits, 0).astype(jnp.int32)


def raised(array, rng, source, target, parts, factor):
    def block_of(axis_at):
        return (jnp.arange(array.shape[axis_at]) // (array.shape[axis_at] // parts)).reshape((-1,) + (1,) * (array.ndim - 1 - axis_at))

    first = jax.random.permutation(rng, parts)[block_of(target)]
    far = (block_of(target) + parts // 2) % parts
    return jnp.where((block_of(source) == first) | (block_of(source) == far), factor * array, array)


def shard_levels(rng, shape, cuts, low, high):
    loudness = 1.0
    for axis_at, shards_of in cuts:
        steps = jax.random.uniform(jax.random.fold_in(jax.random.fold_in(rng, 6), axis_at), (shards_of,), jnp.float32, low / len(cuts), high / len(cuts))
        loudness = loudness * jnp.repeat(jnp.exp(steps), shape[axis_at] // shards_of).reshape((-1,) + (1,) * (len(shape) - 1 - axis_at))
    return loudness


def gaussian_with(own_key, shape, spread, limit, cuts, heavy, held_as=jnp.bfloat16):
    drawn = spread * jax.random.normal(own_key, shape, jnp.float32)
    if cuts:
        drawn = drawn * shard_levels(own_key, shape, cuts, -0.22, 0.18)
    return jnp.clip(raised(drawn, jax.random.fold_in(own_key, 3), *heavy), -limit, limit).astype(held_as)


def setup_inputs(seed: int = 0) -> dict:
    keys = jax.random.split(jax.random.key(seed), 11)
    section_in = draw_section_in(jax.random.fold_in(keys[10], 71), 0)
    fresh = draw_fresh(jax.random.fold_in(keys[10], 71), 0)
    latents = draw_latents(jax.random.fold_in(keys[10], 71), 0)
    image_order = jax.random.permutation(keys[3], IMAGES).astype(jnp.int32)
    token_mask = draw_token_mask(jax.random.fold_in(keys[10], 71), 0)
    norm_gain = jnp.clip(1.0 + 0.1 * jax.random.normal(keys[5], (N_SECTION, D), jnp.float32), 0.5, 1.5).astype(jnp.bfloat16)
    wq = gaussian_with(keys[6], (N_SECTION, D, D), D ** -0.5, 0.1875, ((0, 8), (2, 64)), (1, 2, 64, 4.0))
    wkv = draw_wkv(jax.random.fold_in(keys[10], 71), 0)
    wo = gaussian_with(keys[8], (N_SECTION, D, D), D ** -0.5, 0.1875, ((0, 8), (2, 64)), (1, 2, 64, 4.0))
    alpha = jnp.clip(0.5 + 1.0 * jax.random.uniform(keys[9], (N_SECTION, D), jnp.float32) ** shard_levels(keys[9], (N_SECTION, D), ((0, 8), (1, 64)), -0.2, 0.2), 0.5, 1.5)
    return dict(section_in=section_in, fresh=fresh, latents=latents, image_order=image_order, token_mask=token_mask, norm_gain=norm_gain, wq=wq, wkv=wkv, wo=wo, alpha=alpha)


epsilon = 1e-05
negative_big = -1e+30

def rms_rows(hidden, norm_row):
    hidden32 = hidden.astype(jnp.float32)
    square_mean = lax.optimization_barrier(jnp.mean(hidden32 * hidden32, axis=-1, keepdims=True))
    return (hidden32 * lax.rsqrt(square_mean + epsilon) * norm_row.astype(jnp.float32)).astype(jnp.bfloat16)

def attend(query_heads, key_heads, value_heads, slot_mask):
    scores = jnp.einsum('thd,lhd->htl', query_heads.astype(jnp.float32), key_heads.astype(jnp.float32)) * HD ** (-0.5)
    visible = (jnp.repeat(slot_mask, LAT, axis=1) > 0)[None]
    seen_any = (lax.optimization_barrier(jnp.sum(slot_mask, axis=1)) > 0)[None, :, None]
    largest = lax.optimization_barrier(jnp.max(jnp.where(visible, scores, negative_big), axis=-1, keepdims=True))
    largest = jnp.where(seen_any, largest, 0.0)
    expanded = jnp.where(visible, jnp.exp(jnp.where(visible, scores - largest, 0.0)), 0.0)
    totals = lax.optimization_barrier(jnp.sum(expanded, axis=-1, keepdims=True))
    totals = jnp.where(seen_any, totals, 1.0)
    probs = (expanded / totals).astype(jnp.bfloat16)
    return jnp.einsum('htl,lhd->thd', probs.astype(jnp.float32), value_heads.astype(jnp.float32))

def cross_layer(hidden, norm_row, weight_query, weight_kv, weight_out, gate_row, picked, slot_mask):
    normed = rms_rows(hidden, norm_row)
    queries = jnp.dot(normed, weight_query, preferred_element_type=jnp.float32).astype(jnp.bfloat16)
    flattened = picked.reshape(IMG_MB * LAT, VD)
    key_rows = jnp.dot(flattened, weight_kv[0], preferred_element_type=jnp.float32).astype(jnp.bfloat16)
    values = jnp.dot(flattened, weight_kv[1], preferred_element_type=jnp.float32).astype(jnp.bfloat16)
    attended = attend(queries.reshape(MB, HEADS, HD), key_rows.reshape(-1, HEADS, HD), values.reshape(-1, HEADS, HD), slot_mask)
    attended = attended.reshape(MB, D).astype(jnp.bfloat16)
    projected = jnp.dot(attended, weight_out, preferred_element_type=jnp.float32)
    branch = (projected * jnp.tanh(gate_row.astype(jnp.float32))[None, :]).astype(jnp.bfloat16)
    return (hidden.astype(jnp.float32) + branch.astype(jnp.float32)).astype(jnp.bfloat16)

def reference(section_in, fresh, latents, image_order, token_mask, norm_gain, wq, wkv, wo, alpha):

    def picked_for(micro):
        return latents[image_order[micro * IMG_MB:(micro + 1) * IMG_MB]]

    def run(section, hidden, micro):
        return cross_layer(hidden, norm_gain[section], wq[section], wkv[section], wo[section], alpha[section], picked_for(micro), token_mask[micro])
    first_list = []
    for section in range(N_SECTION):
        first_list.append(run(section, section_in[section], N_SECTION - 1 - section))
    second_list = []
    for section in range(N_SECTION):
        entering = fresh if section == 0 else first_list[section - 1]
        second_list.append(run(section, entering, N_SECTION - section))
    return (jnp.stack(first_list), jnp.stack(second_list))
```

```python
import functools

import jax
import jax.numpy as jnp
from jax import lax
from jax.experimental import pallas as pl
from jax.experimental.pallas import tpu as pltpu
from jax.sharding import PartitionSpec as P

MESH = pl.DeviceIdType.MESH

HD = 128
LAT = 64
IMG = 8
MB = 128
D = 8192
VD = 1280
NY = 4
NZ = 16
QUARTER = D // NY
HALF_VD = VD // 2

epsilon = 1e-05
negative_big = -1e30


def both_ways(edges):
    listed = []
    for reached, via in edges:
        listed.append((reached, via))
        if reached != NZ // 2:
            listed.append((-reached, -via))
    return listed


TREE = both_ways([(6, 0), (2, 0), (1, 0), (3, 2), (4, 2), (8, 6), (7, 6), (5, 6)])
STEPS = sorted({reached - via for reached, via in TREE})


def arrived(ref, sem):
    pltpu.make_async_copy(ref, ref, sem).wait()


class Gather:
    def __init__(self, place, block, send, recv):
        self.place, self.block, self.send, self.recv = place, block, send, recv
        self.copies, self.here = [], {0}

    def need(self, offset):
        if offset not in self.here:
            self.here.add(offset)
            z = self.place[2]
            arrived(self.block(lax.rem(z - offset + NZ, NZ)), self.recv(offset % NZ))

    def pass_on(self, edges):
        s, y, z = self.place
        for reached, via in edges:
            self.need(via)
            ref = self.block(lax.rem(z - via + NZ, NZ))
            copy = pltpu.make_async_remote_copy(
                src_ref=ref,
                dst_ref=ref,
                send_sem=self.send(reached % NZ),
                recv_sem=self.recv(reached % NZ),
                device_id=(s, y * NZ + lax.rem(z + reached - via + NZ, NZ)),
                device_id_type=MESH,
            )
            copy.start()
            self.copies.append(copy)

    def begin(self):
        self.pass_on([edge for edge in TREE if edge[1] == 0])

    def forward(self):
        self.pass_on([edge for edge in TREE if edge[1] != 0])

    def finish(self):
        for reached, _ in TREE:
            self.need(reached)

    def drain(self):
        for copy in self.copies:
            copy.wait_send()


def kernel(
    rows_ref, lat_ref, mask_ref, gain_ref, wq_ref, wkv_ref, wo_ref, alpha_ref,
    out_ref,
    wq_all, wo_all, wkv_all, entry, stripes, columns, first_blocks, blocks, lat_all,
    matrix, squares, partial, others, kv, relay_out, relay_in, out_cols, out_rows, out_pairs,
    local_sem, y_send, y_recv, w_send, w_recv, z_send, z_recv, l_send, l_recv, ly_send, ly_recv,
    c_send, c_recv, r_send, r_recv, n_send, n_recv, oz_send, oz_recv, oy_send, oy_recv,
):
    s = lax.axis_index("section")
    mp = lax.axis_index("mp")
    y, z = mp // NZ, lax.rem(mp, NZ)
    place = (s, y, z)

    def at_y(d):
        return (s, lax.rem(y + d, NY) * NZ + z)

    def at_z(d):
        return (s, y * NZ + lax.rem(z + d + NZ, NZ))

    following = (lax.rem(s + 1, 8), mp)
    previous = (lax.rem(s + 7, 8), mp)

    def send(src, dst, send_sem, recv_sem, device):
        copy = pltpu.make_async_remote_copy(
            src_ref=src, dst_ref=dst, send_sem=send_sem, recv_sem=recv_sem,
            device_id=device, device_id_type=MESH,
        )
        copy.start()
        return copy

    pending = []

    def quarter(ref, which):
        return ref.at[pl.ds(pl.multiple_of(which * QUARTER, QUARTER), QUARTER)]

    keeps = [
        pltpu.make_async_copy(quarter(wq_ref, y), wq_all.at[y], local_sem.at[0]),
        pltpu.make_async_copy(quarter(wo_ref, y), wo_all.at[y], local_sem.at[1]),
        pltpu.make_async_copy(wkv_ref.at[0], wkv_all.at[:, pl.ds(0, HD)], local_sem.at[2]),
        pltpu.make_async_copy(wkv_ref.at[1], wkv_all.at[:, pl.ds(HD, HD)], local_sem.at[3]),
    ]
    for copy in keeps:
        copy.start()

    barrier = pltpu.get_barrier_semaphore()
    greeted = [at_z(d) for d in STEPS] + [at_y(d) for d in (1, 2, 3)] + [following, previous]
    for device in greeted:
        pl.semaphore_signal(barrier, inc=1, device_id=device, device_id_type=MESH)
    pl.semaphore_wait(barrier, len(greeted))

    def entry_rows(which):
        return pl.ds(pl.multiple_of(which * 32, 32), 32)

    def swap_rows(k):
        for d in (2, 1, 3):
            pending.append(
                send(
                    rows_ref.at[k, lax.rem(y + d, NY)], entry.at[k, entry_rows(y)],
                    y_send.at[k, d], y_recv.at[k, d], at_y(d),
                )
            )

    def rows_here(k):
        entry[k, entry_rows(y)] = rows_ref[k, y]
        for d in (1, 2, 3):
            arrived(entry.at[k, entry_rows(lax.rem(y + NY - d, NY))], y_recv.at[k, d])
        for at in range(NZ):
            stripes[k, :, pl.ds(at * 128, 128)] = entry[k, pl.ds(at, 8, stride=NZ), :]

    def swap_weights(k, src, dst):
        for d in (2, 1, 3):
            pending.append(
                send(
                    quarter(src, lax.rem(y + d, NY)), dst.at[y],
                    w_send.at[k, d], w_recv.at[k, d], at_y(d),
                )
            )

    def weights_here(k, dst):
        keeps[k].wait()
        for d in (1, 2, 3):
            arrived(dst.at[lax.rem(y + NY - d, NY)], w_recv.at[k, d])

    swap_rows(0)
    lat_all[0, y, z] = lat_ref[0]
    lat_all[1, y, z] = lat_ref[1]
    lat_gathers = [
        Gather(
            place, lambda at, k=k: lat_all.at[k, y, at],
            lambda i, k=k: l_send.at[k, i], lambda i, k=k: l_recv.at[k, i],
        )
        for k in range(2)
    ]
    lat_gathers[0].begin()
    swap_weights(0, wq_ref, wq_all)

    def spread_lat(k):
        for d in (2, 1, 3):
            pending.append(
                send(
                    lat_all.at[k, y], lat_all.at[k, y],
                    ly_send.at[k, d], ly_recv.at[k, d], at_y(d),
                )
            )

    def lat_here(k):
        for d in (1, 2, 3):
            arrived(lat_all.at[k, lax.rem(y + NY - d, NY)], ly_recv.at[k, d])

    def make_kv(k):
        @pl.loop(0, 4)
        def _(part):
            held = lat_all[k, part].reshape(NZ * 16, HALF_VD)
            low = jnp.dot(held, wkv_all[:HALF_VD, :], preferred_element_type=jnp.float32)
            high = jnp.dot(held, wkv_all[HALF_VD:, :], preferred_element_type=jnp.float32)
            low = low.reshape(NZ, 16, 2 * HD)[:, :8]
            high = high.reshape(NZ, 16, 2 * HD)[:, 8:]
            made = (low + high).reshape(NZ * IMG, 2 * HD).astype(jnp.bfloat16)
            kv[pl.ds(pl.multiple_of(part * 128, 128), 128), :] = made

    gathers = [
        Gather(
            place,
            (lambda at: first_blocks.at[at]) if g == 0 else (lambda at, g=g: blocks.at[g - 1, at]),
            lambda i, g=g: z_send.at[g, i], lambda i, g=g: z_recv.at[g, i],
        )
        for g in range(4)
    ]

    rows_here(0)
    first_blocks[z] = jnp.concatenate(
        [stripes[0, :, pl.ds(0, 1024)], stripes[0, :, pl.ds(1024, 1024)]], axis=0
    ).astype(jnp.bfloat16)
    gathers[0].begin()
    lat_gathers[0].forward()
    swap_rows(1)
    gathers[0].forward()
    lat_gathers[0].finish()
    spread_lat(0)
    swap_weights(1, wo_ref, wo_all)
    gathers[0].finish()
    lat_gathers[1].begin()

    rows_here(1)

    def column_rows(which):
        return pl.ds(pl.multiple_of(which * 8, 8), 8)

    def lanes(which):
        return pl.ds(pl.multiple_of(which * 128, 128), 128)

    def start_columns(k):
        @pl.loop(1, NZ)
        def _(d):
            target = lax.rem(z + d, NZ)
            send(
                stripes.at[k, :, lanes(target)], columns.at[k, column_rows(z)],
                c_send.at[k, d], c_recv.at[k, d], at_z(d),
            )

        columns[k, column_rows(z), :] = stripes[k, :, lanes(z)]

    def columns_here(k):
        @pl.loop(1, NZ)
        def _(d):
            arrived(columns.at[k, column_rows(lax.rem(z + NZ - d, NZ))], c_recv.at[k, d])

    def columns_sent(k):
        @pl.loop(1, NZ)
        def _(d):
            ref = stripes.at[k, :, lanes(lax.rem(z + d, NZ))]
            pltpu.make_async_copy(ref, ref, c_send.at[k, d]).wait()

    gain_here = gain_ref[:, pl.ds(pl.multiple_of(y * QUARTER, QUARTER), QUARTER)]

    def matrix_of_rows():
        @pl.loop(0, NZ // 2)
        def _(pair):
            one = first_blocks[2 * pair].astype(jnp.float32)
            two = first_blocks[2 * pair + 1].astype(jnp.float32)
            total = jnp.zeros((16, 128), jnp.float32)
            where = pl.ds(pl.multiple_of(pair * 16, 16), 16)
            for half in range(2):
                part = jnp.concatenate([one[half * 8:half * 8 + 8], two[half * 8:half * 8 + 8]], axis=0)
                for lane in range(8):
                    cut = part[:, lane * 128:lane * 128 + 128]
                    total = total + cut * cut
                gain_part = gain_here[:, half * 1024:half * 1024 + 1024]
                matrix[where, pl.ds(half * 1024, 1024)] = (part * gain_part).astype(jnp.bfloat16)
            squares[where, :] = total

    def matrix_of_blocks(g):
        squares[...] = jnp.zeros_like(squares)
        for at in range(NZ):
            block = blocks[g - 1, at].astype(jnp.float32)
            squares[...] += block * block
            matrix[:, pl.ds(at * 128, 128)] = (
                block * gain_here[:, at * 128:at * 128 + 128]
            ).astype(jnp.bfloat16)

    def matrix_plain(g):
        for at in range(NZ):
            matrix[:, pl.ds(at * 128, 128)] = blocks[g - 1, at]

    def start_sums(g, weights, with_squares):
        rows = MB + 8 if with_squares else MB
        if with_squares:
            row = jnp.sum(squares[...].T, axis=0, keepdims=True)
            row = jnp.broadcast_to(row, (8, 128))
        for d in (2, 1, 3, 0):
            target = lax.rem(y + d, NY)
            partial[g, target, pl.ds(0, MB), :] = jnp.dot(
                matrix[...], weights[target], preferred_element_type=jnp.float32
            )
            if with_squares:
                partial[g, target, pl.ds(MB, 8), :] = row
            if d:
                pending.append(
                    send(
                        partial.at[g, target, pl.ds(0, rows)], others.at[g, y, pl.ds(0, rows)],
                        r_send.at[g, d], r_recv.at[g, d], at_y(d),
                    )
                )

    def sums(g, with_squares):
        rows = MB + 8 if with_squares else MB
        for d in (1, 2, 3):
            arrived(others.at[g, lax.rem(y + NY - d, NY), pl.ds(0, rows)], r_recv.at[g, d])
        total = partial[g, y, pl.ds(0, rows), :]
        for d in (1, 2, 3):
            total = total + others[g, lax.rem(y + NY - d, NY), pl.ds(0, rows), :]
        return total

    def attend(k, total):
        row = jnp.broadcast_to(total[MB:MB + 1, :], (128, 128))
        scale = lax.rsqrt(row.T * (1.0 / D) + epsilon)
        queries = (total[:MB] * scale).astype(jnp.bfloat16)
        scores = lax.dot_general(
            queries, kv[:, :HD], (((1,), (1,)), ((), ())), preferred_element_type=jnp.float32
        ) * HD ** (-0.5)
        seen = mask_ref[k]
        visible = jnp.concatenate([seen] * 4, axis=1) > 0
        seen_any = jnp.max(seen, axis=1, keepdims=True) > 0
        largest = jnp.max(jnp.where(visible, scores, negative_big), axis=1, keepdims=True)
        largest = jnp.where(seen_any, largest, 0.0)
        expanded = jnp.where(visible, jnp.exp(jnp.where(visible, scores - largest, 0.0)), 0.0)
        totals = jnp.sum(expanded, axis=1, keepdims=True)
        totals = jnp.where(seen_any, totals, 1.0)
        probs = (expanded / totals).astype(jnp.bfloat16)
        return jnp.dot(probs, kv[:, HD:], preferred_element_type=jnp.float32).astype(jnp.bfloat16)

    gate = jnp.tanh(alpha_ref[...])

    def block_out(total, hidden):
        branch = (total * gate).astype(jnp.bfloat16).astype(jnp.float32)
        return (hidden + branch).astype(jnp.bfloat16)

    def start_out(k, made):
        out_cols[k] = made.astype(jnp.float32)

        @pl.loop(1, NZ)
        def _(d):
            send(
                out_cols.at[k, column_rows(lax.rem(z + d, NZ))], out_rows.at[k, column_rows(z)],
                oz_send.at[k, d], oz_recv.at[k, d], at_z(d),
            )

        out_rows[k, column_rows(z), :] = out_cols[k, column_rows(z), :]

    def turn_out(k):
        @pl.loop(1, NZ)
        def _(d):
            arrived(out_rows.at[k, column_rows(lax.rem(z + NZ - d, NZ))], oz_recv.at[k, d])

        for target in range(NY):
            for token in range(2):
                out_pairs[k, target, token] = out_rows[k, pl.ds(2 * target + token, NZ, stride=8), :]
        for d in (2, 1, 3):
            pending.append(
                send(
                    out_pairs.at[k, lax.rem(y + d, NY)], out_ref.at[k, y],
                    oy_send.at[k, d], oy_recv.at[k, d], at_y(d),
                )
            )
        out_ref[k, y] = out_pairs[k, y]

    def out_here(k):
        for d in (1, 2, 3):
            arrived(out_ref.at[k, lax.rem(y + NY - d, NY)], oy_recv.at[k, d])

    def out_sent(k):
        @pl.loop(1, NZ)
        def _(d):
            ref = out_cols.at[k, column_rows(lax.rem(z + d, NZ))]
            pltpu.make_async_copy(ref, ref, oz_send.at[k, d]).wait()

    matrix_of_rows()
    weights_here(0, wq_all)
    start_sums(0, wq_all, True)
    keeps[2].wait()
    keeps[3].wait()
    lat_here(0)
    make_kv(0)
    blocks[0, z] = attend(0, sums(0, True))
    gathers[1].begin()
    lat_gathers[1].forward()
    start_columns(0)
    start_columns(1)
    gathers[1].forward()
    lat_gathers[1].finish()
    spread_lat(1)
    columns_here(0)
    columns_here(1)
    gathers[1].finish()
    matrix_plain(1)
    weights_here(1, wo_all)
    start_sums(1, wo_all, False)
    lat_here(1)
    make_kv(1)
    made = block_out(sums(1, False), columns[0])
    relay_out[...] = made
    pending.append(send(relay_out, relay_in, n_send.at[0], n_recv.at[0], following))
    arrived(relay_in, n_recv.at[0])

    entering = jnp.where(s == 0, columns[1], relay_in[...].astype(jnp.float32))
    blocks[1, z] = entering.astype(jnp.bfloat16)
    gathers[2].begin()
    start_out(0, made)
    gathers[2].forward()
    gathers[2].finish()
    matrix_of_blocks(2)
    start_sums(2, wq_all, True)
    turn_out(0)
    blocks[2, z] = attend(1, sums(2, True))
    gathers[3].begin()
    gathers[3].forward()
    gathers[3].finish()
    matrix_plain(3)
    start_sums(3, wo_all, False)
    start_out(1, block_out(sums(3, False), blocks[1, z].astype(jnp.float32)))
    turn_out(1)
    out_here(0)
    out_here(1)

    for gather in gathers + lat_gathers:
        gather.drain()
    for copy in pending:
        copy.wait_send()
    for k in range(2):
        columns_sent(k)
        out_sent(k)


def local(section_in, fresh, latents, image_order, token_mask, norm_gain, wq, wkv, wo, alpha):
    section = lax.axis_index("section")
    first_micro = 7 - section

    rows = jnp.stack([section_in[0], fresh]).reshape(2, 2, NY, NZ, 128)
    rows = rows.transpose(0, 2, 1, 3, 4).reshape(2, NY, 32, 128).astype(jnp.float32)

    image_ids = lax.dynamic_slice_in_dim(image_order, first_micro * IMG, 2 * IMG)
    picked = jnp.take(latents[:, 0], image_ids, axis=0).reshape(2, IMG, 2, HALF_VD)
    picked = picked.transpose(0, 2, 1, 3).reshape(2, 16, HALF_VD)

    seen = lax.dynamic_slice_in_dim(token_mask, first_micro, 2).reshape(2, NY, NZ, 2, IMG)
    seen = seen.transpose(0, 2, 1, 3, 4).reshape(2, MB, IMG).astype(jnp.float32)
    seen = jnp.tile(seen, (1, 1, 128 // IMG))

    vmem = pl.BlockSpec(memory_space=pltpu.VMEM)
    hbm = pl.BlockSpec(memory_space=pl.ANY)
    bf16, f32 = jnp.bfloat16, jnp.float32
    dma = pltpu.SemaphoreType.DMA
    out = pl.pallas_call(
        kernel,
        out_shape=jax.ShapeDtypeStruct((2, NY, 2, NZ, 128), f32),
        in_specs=[vmem, vmem, vmem, vmem, hbm, hbm, hbm, vmem],
        out_specs=vmem,
        scratch_shapes=[
            pltpu.VMEM((NY, QUARTER, HD), bf16),
            pltpu.VMEM((NY, QUARTER, HD), bf16),
            pltpu.VMEM((VD, 2 * HD), bf16),
            pltpu.VMEM((2, MB, 128), f32),
            pltpu.VMEM((2, 8, QUARTER), f32),
            pltpu.VMEM((2, MB, 128), f32),
            pltpu.VMEM((NZ, 16, 1024), bf16),
            pltpu.VMEM((3, NZ, MB, 128), bf16),
            pltpu.VMEM((2, NY, NZ, 16, HALF_VD), bf16),
            pltpu.VMEM((MB, QUARTER), bf16),
            pltpu.VMEM((MB, 128), f32),
            pltpu.VMEM((4, NY, MB + 8, 128), f32),
            pltpu.VMEM((4, NY, MB + 8, 128), f32),
            pltpu.VMEM((LAT * IMG, 2 * HD), bf16),
            pltpu.VMEM((MB, 128), bf16),
            pltpu.VMEM((MB, 128), bf16),
            pltpu.VMEM((2, MB, 128), f32),
            pltpu.VMEM((2, MB, 128), f32),
            pltpu.VMEM((2, NY, 2, NZ, 128), f32),
            dma((4,)),
            dma((2, 4)), dma((2, 4)),
            dma((2, 4)), dma((2, 4)),
            dma((4, NZ)), dma((4, NZ)),
            dma((2, NZ)), dma((2, NZ)),
            dma((2, 4)), dma((2, 4)),
            dma((2, NZ)), dma((2, NZ)),
            dma((4, 4)), dma((4, 4)),
            dma((1,)), dma((1,)),
            dma((2, NZ)), dma((2, NZ)),
            dma((2, 4)), dma((2, 4)),
        ],
        compiler_params=pltpu.CompilerParams(
            collective_id=0, has_side_effects=True, vmem_limit_bytes=48 * 2**20
        ),
    )(
        rows, picked, seen, norm_gain.astype(f32), wq[0], wkv[0], wo[0], alpha,
    )
    out = out.transpose(0, 2, 1, 3, 4).reshape(2, 1, 2, D).astype(bf16)
    return out[0], out[1]


def solution(mesh):
    in_specs = (
        P("section", "mp", None),
        P("mp", None),
        P(None, "mp", None),
        P(),
        P(),
        P("section", None),
        P("section", None, "mp"),
        P("section", None, None, "mp"),
        P("section", None, "mp"),
        P("section", "mp"),
    )
    out_specs = (P("section", "mp", None), P("section", "mp", None))
    return jax.shard_map(local, mesh=mesh, in_specs=in_specs, out_specs=out_specs, check_vma=False)
```

```python
import functools

import jax
import jax.numpy as jnp
from jax import lax
from jax.experimental import pallas as pl
from jax.experimental.pallas import tpu as pltpu
from jax.sharding import PartitionSpec as P

MESH = pl.DeviceIdType.MESH

HD = 128
LAT = 64
IMG = 8
MB = 128
D = 8192
VD = 1280
NY = 4
NZ = 16
QUARTER = D // NY
HALF_VD = VD // 2

epsilon = 1e-05
negative_big = -1e30


def both_ways(edges):
    listed = []
    for reached, via in edges:
        listed.append((reached, via))
        if reached != NZ // 2:
            listed.append((-reached, -via))
    return listed


TREE = both_ways([(6, 0), (2, 0), (1, 0), (3, 2), (4, 2), (8, 6), (7, 6), (5, 6)])
LEAN = both_ways([(4, 0), (1, 0), (2, 1), (3, 4), (5, 4), (6, 5), (7, 6), (8, 7)])
STEPS = sorted({reached - via for tree in (TREE, LEAN) for reached, via in tree})


def arrived(ref, sem):
    pltpu.make_async_copy(ref, ref, sem).wait()


class Gather:
    def __init__(self, place, block, send, recv, tree):
        self.place, self.block, self.send, self.recv, self.tree = place, block, send, recv, tree
        self.here = {0}

    def origin(self, offset):
        return self.block(lax.rem(self.place[2] - offset + NZ, NZ))

    def need(self, offset):
        if offset not in self.here:
            self.here.add(offset)
            arrived(self.origin(offset), self.recv(offset % NZ))

    def pass_on(self, *vias):
        s, y, z = self.place
        for reached, via in self.tree:
            if abs(via) in vias:
                self.need(via)
                pltpu.make_async_remote_copy(
                    src_ref=self.origin(via),
                    dst_ref=self.origin(via),
                    send_sem=self.send(reached % NZ),
                    recv_sem=self.recv(reached % NZ),
                    device_id=(s, y * NZ + lax.rem(z + reached - via + NZ, NZ)),
                    device_id_type=MESH,
                ).start()

    def finish(self):
        for reached, _ in self.tree:
            self.need(reached)

    def drain(self, first=True):
        for reached, via in self.tree:
            if via or first:
                arrived(self.origin(via), self.send(reached % NZ))


def kernel(
    section_ref, fresh_ref, latents_ref, order_ref, mask_ref, gain_ref, wq_ref, wkv_ref, wo_ref, alpha_ref,
    out_ref,
    wq_all, wo_all, wkv_all, rows32, entry, stripes, columns, first_blocks, blocks, lat_all, seen_all, gain32,
    matrix, squares, partial, others, kv, relay_out, out_cols, out_rows, out_pairs,
    local_sem, y_send, y_recv, w_send, w_recv, z_send, z_recv, l_send, l_recv, ly_send, ly_recv, lr_send, lr_recv,
    c_send, c_recv, r_send, r_recv, n_send, n_recv, k_sem, oz_send, oz_recv, oy_send, oy_recv,
):
    s = lax.axis_index("section")
    mp = lax.axis_index("mp")
    y, z = mp // NZ, lax.rem(mp, NZ)
    place = (s, y, z)

    def at_y(d):
        return (s, lax.rem(y + d, NY) * NZ + z)

    def at_z(d):
        return (s, y * NZ + lax.rem(z + d + NZ, NZ))

    following = (lax.rem(s + 1, 8), mp)
    previous = (lax.rem(s + 7, 8), mp)

    def send(src, dst, send_sem, recv_sem, device):
        copy = pltpu.make_async_remote_copy(
            src_ref=src, dst_ref=dst, send_sem=send_sem, recv_sem=recv_sem,
            device_id=device, device_id_type=MESH,
        )
        copy.start()
        return copy

    pending = []

    def signal(sem, device):
        pl.semaphore_signal(sem, inc=1, device_id=device, device_id_type=MESH)

    def quarter(ref, which):
        return ref.at[pl.ds(pl.multiple_of(which * QUARTER, QUARTER), QUARTER)]

    keeps = [
        pltpu.make_async_copy(quarter(wq_ref, y), wq_all.at[y], local_sem.at[0]),
        pltpu.make_async_copy(quarter(wo_ref, y), wo_all.at[y], local_sem.at[1]),
        pltpu.make_async_copy(wkv_ref.at[0], wkv_all.at[:, pl.ds(0, HD)], local_sem.at[2]),
        pltpu.make_async_copy(wkv_ref.at[1], wkv_all.at[:, pl.ds(HD, HD)], local_sem.at[3]),
    ]
    for copy in keeps:
        copy.start()

    barrier = pltpu.get_barrier_semaphore()
    greeted = [at_z(d) for d in STEPS] + [at_y(d) for d in (1, 2, 3)] + [following, previous]
    for device in greeted:
        signal(barrier, device)

    rows32[0] = section_ref[...].astype(jnp.float32)
    rows32[1] = fresh_ref[...].astype(jnp.float32)
    image_row = lax.broadcasted_iota(jnp.int32, (2 * IMG, 72), 0)
    image_lane = lax.broadcasted_iota(jnp.int32, (2 * IMG, 72), 1)
    chosen = jnp.zeros((2 * IMG, 72), jnp.float32)
    for i in range(2 * IMG):
        image = order_ref[(7 - s) * IMG + i]
        chosen = jnp.where((image_row == i) & (image_lane == image), 1.0, chosen)
    picked = jnp.dot(
        chosen.astype(jnp.bfloat16), latents_ref[...], preferred_element_type=jnp.float32
    )

    def keep_lat(k):
        rows = picked[k * IMG:k * IMG + IMG]
        lat_all[k, z, y] = jnp.concatenate([rows[:, :HALF_VD], rows[:, HALF_VD:]], axis=0).astype(jnp.bfloat16)

    keep_lat(0)

    @pl.when(s == 0)
    def _():
        keep_lat(1)

    pl.semaphore_wait(barrier, len(greeted))

    def swap_rows(k):
        for d in (2, 1, 3):
            target = lax.rem(y + d, NY)
            pending.append(
                send(
                    rows32.at[k, :, pl.ds(pl.multiple_of(target * QUARTER, QUARTER), QUARTER)], entry.at[k, y],
                    y_send.at[k, d], y_recv.at[k, d], at_y(d),
                )
            )

    def rows_here(k):
        entry[k, y] = rows32[k, :, pl.ds(pl.multiple_of(y * QUARTER, QUARTER), QUARTER)]
        for d in (1, 2, 3):
            arrived(entry.at[k, lax.rem(y + NY - d, NY)], y_recv.at[k, d])
        for at in range(NY):
            stripes[k, pl.ds(2 * at, 2), :] = entry[k, at]

    def swap_weights(k, src, dst):
        for d in (2, 1, 3):
            pending.append(
                send(
                    quarter(src, lax.rem(y + d, NY)), dst.at[y],
                    w_send.at[k, d], w_recv.at[k, d], at_y(d),
                )
            )

    def weights_here(k, dst):
        keeps[k].wait()
        for d in (1, 2, 3):
            arrived(dst.at[lax.rem(y + NY - d, NY)], w_recv.at[k, d])

    lat_gathers = [
        Gather(
            place, (lambda at: lat_all.at[1, at, y]) if k else (lambda at: lat_all.at[0, at]),
            lambda i, k=k: l_send.at[k, i], lambda i, k=k: l_recv.at[k, i], TREE if k else LEAN,
        )
        for k in range(2)
    ]

    def lat_part(k, which):
        return lat_all.at[k, :, which] if k else lat_all.at[k, z, which]

    def swap_lat(k):
        for d in (2, 1, 3):
            send(lat_part(k, y), lat_part(k, y), ly_send.at[k, d], ly_recv.at[k, d], at_y(d))

    def lat_swapped(k):
        for d in (1, 2, 3):
            arrived(lat_part(k, lax.rem(y + NY - d, NY)), ly_recv.at[k, d])

    def lat_swap_sent(k):
        for d in (1, 2, 3):
            arrived(lat_part(k, y), ly_send.at[k, d])

    swap_rows(0)
    swap_lat(0)
    swap_weights(0, wq_ref, wq_all)
    gain32[...] = gain_ref[...].astype(jnp.float32)

    row_at = lax.broadcasted_iota(jnp.int32, (MB, MB), 0)
    lane_at = lax.broadcasted_iota(jnp.int32, (MB, MB), 1)
    token = ((row_at >> 1) & 3) * 32 + (row_at >> 3) * 2 + (row_at & 1)
    reorder = jnp.where(lane_at == token, 1.0, 0.0).astype(jnp.bfloat16)
    slot_at = lax.broadcasted_iota(jnp.int32, (IMG, MB), 0)
    slot_lane = lax.broadcasted_iota(jnp.int32, (IMG, MB), 1)
    repeat = jnp.where((slot_lane & 7) == slot_at, 1.0, 0.0).astype(jnp.bfloat16)
    for k in range(2):
        slots = mask_ref[7 - s + k].astype(jnp.float32).astype(jnp.bfloat16)
        slots = lax.dot_general(
            reorder, slots, (((1,), (1,)), ((), ())), preferred_element_type=jnp.float32
        )
        seen_all[k] = jnp.dot(slots.astype(jnp.bfloat16), repeat, preferred_element_type=jnp.float32)

    def make_kv(k):
        @pl.loop(0, 4)
        def _(part):
            held = lat_all[k, pl.ds(part * 4, 4)].reshape(NZ * 16, HALF_VD)
            low = jnp.dot(held, wkv_all[:HALF_VD, :], preferred_element_type=jnp.float32)
            high = jnp.dot(held, wkv_all[HALF_VD:, :], preferred_element_type=jnp.float32)
            low = low.reshape(NZ, 16, 2 * HD)[:, :8]
            high = high.reshape(NZ, 16, 2 * HD)[:, 8:]
            made = (low + high).reshape(NZ * IMG, 2 * HD).astype(jnp.bfloat16)
            kv[pl.ds(pl.multiple_of(part * 128, 128), 128), :] = made

    gathers = [
        Gather(
            place,
            (lambda at: first_blocks.at[at]) if g == 0 else (lambda at, g=g: blocks.at[g - 1, at]),
            lambda i, g=g: z_send.at[g, i], lambda i, g=g: z_recv.at[g, i], TREE,
        )
        for g in range(4)
    ]

    rows_here(0)
    first_blocks[z] = jnp.concatenate(
        [stripes[0, :, pl.ds(0, 1024)], stripes[0, :, pl.ds(1024, 1024)]], axis=0
    ).astype(jnp.bfloat16)
    gathers[0].pass_on(0)
    lat_swapped(0)
    lat_gathers[0].pass_on(0)
    swap_rows(1)
    gathers[0].pass_on(2, 6)
    lat_gathers[0].pass_on(1, 4)
    rows_here(1)
    gathers[0].finish()
    signal(k_sem, previous)
    lat_gathers[0].pass_on(5)

    def column_rows(which):
        return pl.ds(pl.multiple_of(which * 8, 8), 8)

    def lanes(which):
        return pl.ds(pl.multiple_of(which * 128, 128), 128)

    def start_columns(k):
        @pl.loop(1, NZ)
        def _(d):
            target = lax.rem(z + d, NZ)
            send(
                stripes.at[k, :, lanes(target)], columns.at[k, column_rows(z)],
                c_send.at[k, d], c_recv.at[k, d], at_z(d),
            )

        columns[k, column_rows(z), :] = stripes[k, :, lanes(z)]

    def columns_here(k):
        @pl.loop(1, NZ)
        def _(d):
            arrived(columns.at[k, column_rows(lax.rem(z + NZ - d, NZ))], c_recv.at[k, d])

    def columns_sent(k):
        @pl.loop(1, NZ)
        def _(d):
            ref = stripes.at[k, :, lanes(lax.rem(z + d, NZ))]
            pltpu.make_async_copy(ref, ref, c_send.at[k, d]).wait()

    gain_here = gain32[:, pl.ds(pl.multiple_of(y * QUARTER, QUARTER), QUARTER)]

    def matrix_of_rows():
        @pl.loop(0, NZ // 2)
        def _(pair):
            one = first_blocks[2 * pair].astype(jnp.float32)
            two = first_blocks[2 * pair + 1].astype(jnp.float32)
            total = jnp.zeros((16, 128), jnp.float32)
            where = pl.ds(pl.multiple_of(pair * 16, 16), 16)
            for half in range(2):
                part = jnp.concatenate([one[half * 8:half * 8 + 8], two[half * 8:half * 8 + 8]], axis=0)
                for lane in range(8):
                    cut = part[:, lane * 128:lane * 128 + 128]
                    total = total + cut * cut
                gain_part = gain_here[:, half * 1024:half * 1024 + 1024]
                matrix[where, pl.ds(half * 1024, 1024)] = (part * gain_part).astype(jnp.bfloat16)
            squares[where, :] = total

    def matrix_of_blocks(g):
        squares[...] = jnp.zeros_like(squares)
        for at in range(NZ):
            block = blocks[g - 1, at].astype(jnp.float32)
            squares[...] += block * block
            matrix[:, pl.ds(at * 128, 128)] = (
                block * gain_here[:, at * 128:at * 128 + 128]
            ).astype(jnp.bfloat16)

    def matrix_plain(g):
        for at in range(NZ):
            matrix[:, pl.ds(at * 128, 128)] = blocks[g - 1, at]

    def start_sums(g, weights, with_squares):
        rows = MB + 8 if with_squares else MB
        if with_squares:
            row = jnp.sum(squares[...].T, axis=0, keepdims=True)
            row = jnp.broadcast_to(row, (8, 128))
        for d in (2, 1, 3, 0):
            target = lax.rem(y + d, NY)
            partial[g, target, pl.ds(0, MB), :] = jnp.dot(
                matrix[...], weights[target], preferred_element_type=jnp.float32
            )
            if with_squares:
                partial[g, target, pl.ds(MB, 8), :] = row
            if d:
                pending.append(
                    send(
                        partial.at[g, target, pl.ds(0, rows)], others.at[g, y, pl.ds(0, rows)],
                        r_send.at[g, d], r_recv.at[g, d], at_y(d),
                    )
                )

    def sums(g, with_squares):
        rows = MB + 8 if with_squares else MB
        for d in (1, 2, 3):
            arrived(others.at[g, lax.rem(y + NY - d, NY), pl.ds(0, rows)], r_recv.at[g, d])
        total = partial[g, y, pl.ds(0, rows), :]
        for d in (1, 2, 3):
            total = total + others[g, lax.rem(y + NY - d, NY), pl.ds(0, rows), :]
        return total

    def attend(k, total):
        row = jnp.broadcast_to(total[MB:MB + 1, :], (128, 128))
        scale = lax.rsqrt(row.T * (1.0 / D) + epsilon)
        queries = (total[:MB] * scale).astype(jnp.bfloat16)
        scores = lax.dot_general(
            queries, kv[:, :HD], (((1,), (1,)), ((), ())), preferred_element_type=jnp.float32
        ) * HD ** (-0.5)
        seen = seen_all[k]
        visible = jnp.concatenate([seen] * 4, axis=1) > 0
        seen_any = jnp.max(seen, axis=1, keepdims=True) > 0
        largest = jnp.max(jnp.where(visible, scores, negative_big), axis=1, keepdims=True)
        largest = jnp.where(seen_any, largest, 0.0)
        expanded = jnp.where(visible, jnp.exp(jnp.where(visible, scores - largest, 0.0)), 0.0)
        totals = jnp.sum(expanded, axis=1, keepdims=True)
        totals = jnp.where(seen_any, totals, 1.0)
        probs = (expanded / totals).astype(jnp.bfloat16)
        return jnp.dot(probs, kv[:, HD:], preferred_element_type=jnp.float32).astype(jnp.bfloat16)

    gate = jnp.tanh(alpha_ref[...])

    def block_out(total, hidden):
        branch = (total * gate).astype(jnp.bfloat16).astype(jnp.float32)
        return (hidden + branch).astype(jnp.bfloat16)

    def start_out(k, made):
        out_cols[k] = made.astype(jnp.float32)

        @pl.loop(1, NZ)
        def _(d):
            send(
                out_cols.at[k, column_rows(lax.rem(z + d, NZ))], out_rows.at[k, column_rows(z)],
                oz_send.at[k, d], oz_recv.at[k, d], at_z(d),
            )

        out_rows[k, column_rows(z), :] = out_cols[k, column_rows(z), :]

    def turn_out(k):
        @pl.loop(1, NZ)
        def _(d):
            arrived(out_rows.at[k, column_rows(lax.rem(z + NZ - d, NZ))], oz_recv.at[k, d])

        for target in range(NY):
            for token in range(2):
                out_pairs[k, target, token] = out_rows[k, pl.ds(2 * target + token, NZ, stride=8), :]
        for d in (2, 1, 3):
            pending.append(
                send(
                    out_pairs.at[k, lax.rem(y + d, NY)], out_ref.at[k, y],
                    oy_send.at[k, d], oy_recv.at[k, d], at_y(d),
                )
            )
        out_ref[k, y] = out_pairs[k, y]

    def out_here(k):
        for d in (1, 2, 3):
            arrived(out_ref.at[k, lax.rem(y + NY - d, NY)], oy_recv.at[k, d])

    def out_sent(k):
        @pl.loop(1, NZ)
        def _(d):
            ref = out_cols.at[k, column_rows(lax.rem(z + d, NZ))]
            pltpu.make_async_copy(ref, ref, oz_send.at[k, d]).wait()

    matrix_of_rows()
    weights_here(0, wq_all)
    start_sums(0, wq_all, True)
    swap_weights(1, wo_ref, wo_all)
    lat_gathers[0].pass_on(6, 7)
    keeps[2].wait()
    keeps[3].wait()
    lat_gathers[0].finish()
    make_kv(0)
    blocks[0, z] = attend(0, sums(0, True))
    gathers[1].pass_on(0)

    @pl.when(s < 7)
    def _():
        send(lat_all.at[0], lat_all.at[1], lr_send.at[0], lr_recv.at[0], following)

    start_columns(0)
    start_columns(1)

    @pl.when(s == 0)
    def _():
        lat_gathers[1].pass_on(0)

    gathers[1].pass_on(2, 6)
    columns_here(0)
    columns_here(1)
    gathers[1].finish()

    @pl.when(s == 0)
    def _():
        lat_gathers[1].pass_on(2, 6)

    matrix_plain(1)
    weights_here(1, wo_all)
    start_sums(1, wo_all, False)
    pl.semaphore_wait(k_sem, 1)

    @pl.when(s == 0)
    def _():
        lat_gathers[1].finish()

    made = block_out(sums(1, False), columns[0])
    relay_out[...] = made

    hops = [reached for reached, via in TREE if via == 0]

    @pl.when(s < 7)
    def _():
        for hop in hops:
            send(
                relay_out, blocks.at[1, z], z_send.at[2, hop % NZ], z_recv.at[2, hop % NZ],
                (s + 1, y * NZ + lax.rem(z + hop + NZ, NZ)),
            )
        send(relay_out, blocks.at[1, z], n_send.at[0], n_recv.at[0], following)

    @pl.when(s == 0)
    def _():
        blocks[1, z] = columns[1].astype(jnp.bfloat16)
        for hop in hops:
            send(
                blocks.at[1, z], blocks.at[1, z], z_send.at[3, hop % NZ], z_recv.at[2, hop % NZ],
                at_z(hop),
            )

    start_out(0, made)

    @pl.when(s == 0)
    def _():
        swap_lat(1)

    gathers[2].pass_on(2, 6)

    @pl.when(s > 0)
    def _():
        arrived(blocks.at[1, z], n_recv.at[0])

    gathers[2].finish()
    matrix_of_blocks(2)
    start_sums(2, wq_all, True)

    turn_out(0)

    @pl.when(s == 0)
    def _():
        lat_swapped(1)

    @pl.when(s > 0)
    def _():
        arrived(lat_all.at[1], lr_recv.at[0])

    make_kv(1)
    blocks[2, z] = attend(1, sums(2, True))

    @pl.when(s == 0)
    def _():
        for hop in hops:
            arrived(blocks.at[1, z], z_send.at[3, hop % NZ])

    gathers[3].pass_on(0)
    gathers[3].pass_on(2, 6)
    gathers[3].finish()
    matrix_plain(3)
    start_sums(3, wo_all, False)
    start_out(1, block_out(sums(3, False), blocks[1, z].astype(jnp.float32)))
    turn_out(1)
    out_here(0)
    out_here(1)

    gathers[0].drain()
    gathers[1].drain()
    gathers[2].drain(False)
    gathers[3].drain()
    lat_gathers[0].drain()
    lat_swap_sent(0)

    @pl.when(s == 0)
    def _():
        lat_swap_sent(1)
        lat_gathers[1].drain()

    @pl.when(s < 7)
    def _():
        for hop in hops:
            arrived(relay_out, z_send.at[2, hop % NZ])
        arrived(relay_out, n_send.at[0])
        arrived(lat_all.at[0], lr_send.at[0])

    for copy in pending:
        copy.wait_send()
    for k in range(2):
        columns_sent(k)
        out_sent(k)


def local(section_in, fresh, latents, image_order, token_mask, norm_gain, wq, wkv, wo, alpha):
    vmem = pl.BlockSpec(memory_space=pltpu.VMEM)
    smem = pl.BlockSpec(memory_space=pltpu.SMEM)
    hbm = pl.BlockSpec(memory_space=pl.ANY)
    bf16, f32 = jnp.bfloat16, jnp.float32
    dma = pltpu.SemaphoreType.DMA
    out = pl.pallas_call(
        kernel,
        out_shape=jax.ShapeDtypeStruct((2, NY, 2, NZ, 128), f32),
        in_specs=[vmem, vmem, vmem, smem, vmem, vmem, hbm, hbm, hbm, vmem],
        out_specs=vmem,
        scratch_shapes=[
            pltpu.VMEM((NY, QUARTER, HD), bf16),
            pltpu.VMEM((NY, QUARTER, HD), bf16),
            pltpu.VMEM((VD, 2 * HD), bf16),
            pltpu.VMEM((2, 2, D), f32),
            pltpu.VMEM((2, NY, 2, QUARTER), f32),
            pltpu.VMEM((2, 8, QUARTER), f32),
            pltpu.VMEM((2, MB, 128), f32),
            pltpu.VMEM((NZ, 16, 1024), bf16),
            pltpu.VMEM((3, NZ, MB, 128), bf16),
            pltpu.VMEM((2, NZ, NY, 16, HALF_VD), bf16),
            pltpu.VMEM((2, MB, 128), f32),
            pltpu.VMEM((1, D), f32),
            pltpu.VMEM((MB, QUARTER), bf16),
            pltpu.VMEM((MB, 128), f32),
            pltpu.VMEM((4, NY, MB + 8, 128), f32),
            pltpu.VMEM((4, NY, MB + 8, 128), f32),
            pltpu.VMEM((LAT * IMG, 2 * HD), bf16),
            pltpu.VMEM((MB, 128), bf16),
            pltpu.VMEM((2, MB, 128), f32),
            pltpu.VMEM((2, MB, 128), f32),
            pltpu.VMEM((2, NY, 2, NZ, 128), f32),
            dma((4,)),
            dma((2, 4)), dma((2, 4)),
            dma((2, 4)), dma((2, 4)),
            dma((4, NZ)), dma((4, NZ)),
            dma((2, NZ)), dma((2, NZ)),
            dma((2, 4)), dma((2, 4)),
            dma((1,)), dma((1,)),
            dma((2, NZ)), dma((2, NZ)),
            dma((4, 4)), dma((4, 4)),
            dma((1,)), dma((1,)),
            pltpu.SemaphoreType.REGULAR,
            dma((2, NZ)), dma((2, NZ)),
            dma((2, 4)), dma((2, 4)),
        ],
        compiler_params=pltpu.CompilerParams(
            collective_id=0, has_side_effects=True, vmem_limit_bytes=62 * 2**20
        ),
    )(
        section_in[0], fresh, latents.reshape(72, VD), image_order, token_mask.transpose(0, 2, 1), norm_gain,
        wq[0], wkv[0], wo[0], alpha,
    )
    out = out.transpose(0, 2, 1, 3, 4).reshape(2, 1, 2, D).astype(bf16)
    return out[0], out[1]


def solution(mesh):
    in_specs = (
        P("section", "mp", None),
        P("mp", None),
        P(None, "mp", None),
        P(),
        P(),
        P("section", None),
        P("section", None, "mp"),
        P("section", None, None, "mp"),
        P("section", None, "mp"),
        P("section", "mp"),
    )
    out_specs = (P("section", "mp", None), P("section", "mp", None))
    return jax.shard_map(local, mesh=mesh, in_specs=in_specs, out_specs=out_specs, check_vma=False)
```

```python
import functools

import jax
import jax.numpy as jnp
from jax import lax
from jax.experimental import pallas as pl
from jax.experimental.pallas import tpu as pltpu
from jax.sharding import PartitionSpec as P

MESH = pl.DeviceIdType.MESH

HD = 128
LAT = 64
IMG = 8
MB = 128
D = 8192
VD = 1280
NY = 4
NZ = 16
QUARTER = D // NY
HALF_VD = VD // 2

epsilon = 1e-05
negative_big = -1e30


def both_ways(edges):
    listed = []
    for reached, via in edges:
        listed.append((reached, via))
        if reached != NZ // 2:
            listed.append((-reached, -via))
    return listed


TREE = both_ways([(6, 0), (2, 0), (1, 0), (3, 2), (4, 2), (8, 6), (7, 6), (5, 6)])
LEAN = both_ways([(3, 0), (1, 0), (6, 3), (4, 3), (2, 3), (7, 6), (5, 6), (8, 6)])
STEPS = sorted({reached - via for tree in (TREE, LEAN) for reached, via in tree})


def arrived(ref, sem):
    pltpu.make_async_copy(ref, ref, sem).wait()


class Gather:
    def __init__(self, place, block, send, recv, tree):
        self.place, self.block, self.send, self.recv, self.tree = place, block, send, recv, tree
        self.here = {0}

    def origin(self, offset):
        return self.block(lax.rem(self.place[2] - offset + NZ, NZ))

    def need(self, offset):
        if offset not in self.here:
            self.here.add(offset)
            arrived(self.origin(offset), self.recv(offset % NZ))

    def pass_on(self, *vias):
        s, y, z = self.place
        for reached, via in self.tree:
            if abs(via) in vias:
                self.need(via)
                pltpu.make_async_remote_copy(
                    src_ref=self.origin(via),
                    dst_ref=self.origin(via),
                    send_sem=self.send(reached % NZ),
                    recv_sem=self.recv(reached % NZ),
                    device_id=(s, y * NZ + lax.rem(z + reached - via + NZ, NZ)),
                    device_id_type=MESH,
                ).start()

    def finish(self):
        for reached, _ in self.tree:
            self.need(reached)

    def drain(self, first=True):
        for reached, via in self.tree:
            if via or first:
                arrived(self.origin(via), self.send(reached % NZ))


def kernel(
    section_ref, fresh_ref, latents_ref, order_ref, mask_ref, gain_ref, wq_ref, wkv_ref, wo_ref, alpha_ref,
    out_ref,
    wq_all, wo_all, wkv_all, rows32, entry, stripes, columns, first_blocks, blocks, lat_all, seen_all, gain32,
    matrix, squares, partial, others, kv, relay_out, out_cols, out_rows, out_pairs, gates, split_out, split_in, entered,
    local_sem, y_send, y_recv, w_send, w_recv, z_send, z_recv, l_send, l_recv, ly_send, ly_recv, lr_send, lr_recv,
    c_send, c_recv, r_send, r_recv, n_send, n_recv, k_sem, oz_send, oz_recv, oy_send, oy_recv, g_send, g_recv, h_send, h_recv,
):
    s = lax.axis_index("section")
    mp = lax.axis_index("mp")
    y, z = mp // NZ, lax.rem(mp, NZ)
    place = (s, y, z)

    def at_y(d):
        return (s, lax.rem(y + d, NY) * NZ + z)

    def at_z(d):
        return (s, y * NZ + lax.rem(z + d + NZ, NZ))

    following = (lax.rem(s + 1, 8), mp)
    previous = (lax.rem(s + 7, 8), mp)

    def send(src, dst, send_sem, recv_sem, device):
        copy = pltpu.make_async_remote_copy(
            src_ref=src, dst_ref=dst, send_sem=send_sem, recv_sem=recv_sem,
            device_id=device, device_id_type=MESH,
        )
        copy.start()
        return copy

    pending = []

    def signal(sem, device):
        pl.semaphore_signal(sem, inc=1, device_id=device, device_id_type=MESH)

    def quarter(ref, which):
        return ref.at[pl.ds(pl.multiple_of(which * QUARTER, QUARTER), QUARTER)]

    keeps = [
        pltpu.make_async_copy(quarter(wq_ref, y), wq_all.at[y], local_sem.at[0]),
        pltpu.make_async_copy(quarter(wo_ref, y), wo_all.at[y], local_sem.at[1]),
        pltpu.make_async_copy(wkv_ref.at[0], wkv_all.at[:, pl.ds(0, HD)], local_sem.at[2]),
        pltpu.make_async_copy(wkv_ref.at[1], wkv_all.at[:, pl.ds(HD, HD)], local_sem.at[3]),
    ]
    for copy in keeps:
        copy.start()

    barrier = pltpu.get_barrier_semaphore()
    greeted = [at_z(d) for d in STEPS] + [at_y(d) for d in (1, 2, 3)] + [following, previous]
    for device in greeted:
        signal(barrier, device)

    rows32[0] = section_ref[...].astype(jnp.float32)
    rows32[1] = fresh_ref[...].astype(jnp.float32)
    image_row = lax.broadcasted_iota(jnp.int32, (2 * IMG, 72), 0)
    image_lane = lax.broadcasted_iota(jnp.int32, (2 * IMG, 72), 1)
    chosen = jnp.zeros((2 * IMG, 72), jnp.float32)
    for i in range(2 * IMG):
        image = order_ref[(7 - s) * IMG + i]
        chosen = jnp.where((image_row == i) & (image_lane == image), 1.0, chosen)
    picked = jnp.dot(
        chosen.astype(jnp.bfloat16), latents_ref[...], preferred_element_type=jnp.float32
    )

    def keep_lat(k):
        rows = picked[k * IMG:k * IMG + IMG]
        lat_all[k, z, y] = jnp.concatenate([rows[:, :HALF_VD], rows[:, HALF_VD:]], axis=0).astype(jnp.bfloat16)

    keep_lat(0)

    @pl.when(s == 0)
    def _():
        keep_lat(1)

    pl.semaphore_wait(barrier, len(greeted))

    def swap_rows(k):
        for d in (2, 1, 3):
            target = lax.rem(y + d, NY)
            pending.append(
                send(
                    rows32.at[k, :, pl.ds(pl.multiple_of(target * QUARTER, QUARTER), QUARTER)], entry.at[k, y],
                    y_send.at[k, d], y_recv.at[k, d], at_y(d),
                )
            )

    def rows_here(k):
        entry[k, y] = rows32[k, :, pl.ds(pl.multiple_of(y * QUARTER, QUARTER), QUARTER)]
        for d in (1, 2, 3):
            arrived(entry.at[k, lax.rem(y + NY - d, NY)], y_recv.at[k, d])
        for at in range(NY):
            stripes[k, pl.ds(2 * at, 2), :] = entry[k, at]

    def swap_weights(k, src, dst):
        for d in (2, 1, 3):
            pending.append(
                send(
                    quarter(src, lax.rem(y + d, NY)), dst.at[y],
                    w_send.at[k, d], w_recv.at[k, d], at_y(d),
                )
            )

    def swap_part(k, start, count):
        for d in (2, 1, 3):
            pending.append(
                send(
                    wo_ref.at[pl.ds(pl.multiple_of(lax.rem(y + d, NY) * QUARTER + start, 16), count)],
                    wo_all.at[y, pl.ds(start, count)],
                    w_send.at[k, d], w_recv.at[k, d], at_y(d),
                )
            )

    def part_here(k, start, count):
        for d in (1, 2, 3):
            arrived(wo_all.at[lax.rem(y + NY - d, NY), pl.ds(start, count)], w_recv.at[k, d])

    def weights_here(k, dst):
        keeps[k].wait()
        for d in (1, 2, 3):
            arrived(dst.at[lax.rem(y + NY - d, NY)], w_recv.at[k, d])

    lat_gathers = [
        Gather(
            place, (lambda at: lat_all.at[1, at, y]) if k else (lambda at: lat_all.at[0, at]),
            lambda i, k=k: l_send.at[k, i], lambda i, k=k: l_recv.at[k, i], TREE if k else LEAN,
        )
        for k in range(2)
    ]

    def lat_part(k, which):
        return lat_all.at[k, :, which] if k else lat_all.at[k, z, which]

    def swap_lat(k):
        for d in (2, 1, 3):
            send(lat_part(k, y), lat_part(k, y), ly_send.at[k, d], ly_recv.at[k, d], at_y(d))

    def lat_swapped(k):
        for d in (1, 2, 3):
            arrived(lat_part(k, lax.rem(y + NY - d, NY)), ly_recv.at[k, d])

    def lat_swap_sent(k):
        for d in (1, 2, 3):
            arrived(lat_part(k, y), ly_send.at[k, d])

    gates[y] = jnp.broadcast_to(jnp.tanh(alpha_ref[...]), (8, 128))
    swap_rows(0)
    swap_lat(0)
    for d in (2, 1, 3):
        pending.append(send(gates.at[y], gates.at[y], g_send.at[d], g_recv.at[d], at_y(d)))
    swap_rows(1)
    swap_weights(0, wq_ref, wq_all)
    swap_part(1, 0, 512)
    gain32[...] = gain_ref[...].astype(jnp.float32)

    row_at = lax.broadcasted_iota(jnp.int32, (MB, MB), 0)
    lane_at = lax.broadcasted_iota(jnp.int32, (MB, MB), 1)
    token = ((row_at >> 1) & 3) * 32 + (row_at >> 3) * 2 + (row_at & 1)
    reorder = jnp.where(lane_at == token, 1.0, 0.0).astype(jnp.bfloat16)
    slot_at = lax.broadcasted_iota(jnp.int32, (IMG, MB), 0)
    slot_lane = lax.broadcasted_iota(jnp.int32, (IMG, MB), 1)
    repeat = jnp.where((slot_lane & 7) == slot_at, 1.0, 0.0).astype(jnp.bfloat16)
    for k in range(2):
        slots = mask_ref[7 - s + k].astype(jnp.float32).astype(jnp.bfloat16)
        slots = lax.dot_general(
            reorder, slots, (((1,), (1,)), ((), ())), preferred_element_type=jnp.float32
        )
        seen_all[k] = jnp.dot(slots.astype(jnp.bfloat16), repeat, preferred_element_type=jnp.float32)

    def make_kv(k):
        @pl.loop(0, 4)
        def _(part):
            held = lat_all[k, pl.ds(part * 4, 4)].reshape(NZ * 16, HALF_VD)
            low = jnp.dot(held, wkv_all[:HALF_VD, :], preferred_element_type=jnp.float32)
            high = jnp.dot(held, wkv_all[HALF_VD:, :], preferred_element_type=jnp.float32)
            low = low.reshape(NZ, 16, 2 * HD)[:, :8]
            high = high.reshape(NZ, 16, 2 * HD)[:, 8:]
            made = (low + high).reshape(NZ * IMG, 2 * HD).astype(jnp.bfloat16)
            kv[pl.ds(pl.multiple_of(part * 128, 128), 128), :] = made

    gathers = [
        Gather(
            place,
            (lambda at: first_blocks.at[at]) if g == 0 else (lambda at, g=g: blocks.at[g - 1, at]),
            lambda i, g=g: z_send.at[g, i], lambda i, g=g: z_recv.at[g, i], TREE,
        )
        for g in range(4)
    ]

    rows_here(0)
    first_blocks[z] = jnp.concatenate(
        [stripes[0, :, pl.ds(0, 1024)], stripes[0, :, pl.ds(1024, 1024)]], axis=0
    ).astype(jnp.bfloat16)
    gathers[0].pass_on(0)
    lat_swapped(0)
    lat_gathers[0].pass_on(0)
    gathers[0].pass_on(2, 6)
    lat_gathers[0].pass_on(3)
    rows_here(1)
    gathers[0].finish()
    signal(k_sem, previous)
    lat_gathers[0].pass_on(6)

    def column_rows(which):
        return pl.ds(pl.multiple_of(which * 8, 8), 8)

    def lanes(which):
        return pl.ds(pl.multiple_of(which * 128, 128), 128)

    def start_columns(k):
        @pl.loop(1, NZ)
        def _(d):
            target = lax.rem(z + d, NZ)
            send(
                stripes.at[k, :, lanes(target)], columns.at[k, column_rows(z)],
                c_send.at[k, d], c_recv.at[k, d], at_z(d),
            )

        columns[k, column_rows(z), :] = stripes[k, :, lanes(z)]

    def columns_here(k):
        @pl.loop(1, NZ)
        def _(d):
            arrived(columns.at[k, column_rows(lax.rem(z + NZ - d, NZ))], c_recv.at[k, d])

    def columns_sent(k):
        @pl.loop(1, NZ)
        def _(d):
            ref = stripes.at[k, :, lanes(lax.rem(z + d, NZ))]
            pltpu.make_async_copy(ref, ref, c_send.at[k, d]).wait()

    gain_here = gain32[:, pl.ds(pl.multiple_of(y * QUARTER, QUARTER), QUARTER)]

    def matrix_of_rows():
        @pl.loop(0, NZ // 2)
        def _(pair):
            one = first_blocks[2 * pair].astype(jnp.float32)
            two = first_blocks[2 * pair + 1].astype(jnp.float32)
            total = jnp.zeros((16, 128), jnp.float32)
            where = pl.ds(pl.multiple_of(pair * 16, 16), 16)
            for half in range(2):
                part = jnp.concatenate([one[half * 8:half * 8 + 8], two[half * 8:half * 8 + 8]], axis=0)
                for lane in range(8):
                    cut = part[:, lane * 128:lane * 128 + 128]
                    total = total + cut * cut
                gain_part = gain_here[:, half * 1024:half * 1024 + 1024]
                matrix[where, pl.ds(half * 1024, 1024)] = (part * gain_part).astype(jnp.bfloat16)
            squares[where, :] = total

    def matrix_of_blocks(g):
        squares[...] = jnp.zeros_like(squares)
        for at in range(NZ):
            block = blocks[g - 1, at].astype(jnp.float32)
            squares[...] += block * block
            matrix[:, pl.ds(at * 128, 128)] = (
                block * gain_here[:, at * 128:at * 128 + 128]
            ).astype(jnp.bfloat16)

    def matrix_plain(g):
        for at in range(NZ):
            matrix[:, pl.ds(at * 128, 128)] = blocks[g - 1, at]

    def start_sums(g, weights, with_squares):
        rows = MB + 8 if with_squares else MB
        if with_squares:
            row = jnp.sum(squares[...].T, axis=0, keepdims=True)
            row = jnp.broadcast_to(row, (8, 128))
        for d in (2, 1, 3, 0):
            target = lax.rem(y + d, NY)
            partial[g, target, pl.ds(0, MB), :] = jnp.dot(
                matrix[...], weights[target], preferred_element_type=jnp.float32
            )
            if with_squares:
                partial[g, target, pl.ds(MB, 8), :] = row
            if d:
                pending.append(
                    send(
                        partial.at[g, target, pl.ds(0, rows)], others.at[g, y, pl.ds(0, rows)],
                        r_send.at[g, d], r_recv.at[g, d], at_y(d),
                    )
                )

    def sums(g, with_squares):
        rows = MB + 8 if with_squares else MB
        for d in (1, 2, 3):
            arrived(others.at[g, lax.rem(y + NY - d, NY), pl.ds(0, rows)], r_recv.at[g, d])
        total = partial[g, y, pl.ds(0, rows), :]
        for d in (1, 2, 3):
            total = total + others[g, lax.rem(y + NY - d, NY), pl.ds(0, rows), :]
        return total

    def attend(k, total):
        row = jnp.broadcast_to(total[MB:MB + 1, :], (128, 128))
        scale = lax.rsqrt(row.T * (1.0 / D) + epsilon)
        queries = (total[:MB] * scale).astype(jnp.bfloat16)
        scores = lax.dot_general(
            queries, kv[:, :HD], (((1,), (1,)), ((), ())), preferred_element_type=jnp.float32
        ) * HD ** (-0.5)
        seen = seen_all[k]
        visible = jnp.concatenate([seen] * 4, axis=1) > 0
        seen_any = jnp.max(seen, axis=1, keepdims=True) > 0
        largest = jnp.max(jnp.where(visible, scores, negative_big), axis=1, keepdims=True)
        largest = jnp.where(seen_any, largest, 0.0)
        expanded = jnp.where(visible, jnp.exp(jnp.where(visible, scores - largest, 0.0)), 0.0)
        totals = jnp.sum(expanded, axis=1, keepdims=True)
        totals = jnp.where(seen_any, totals, 1.0)
        probs = (expanded / totals).astype(jnp.bfloat16)
        return jnp.dot(probs, kv[:, HD:], preferred_element_type=jnp.float32).astype(jnp.bfloat16)

    gate = jnp.tanh(alpha_ref[...])

    def block_out(total, hidden):
        branch = (total * gate).astype(jnp.bfloat16).astype(jnp.float32)
        return (hidden + branch).astype(jnp.bfloat16)

    def start_out(k, made):
        out_cols[k] = made.astype(jnp.float32)
        send_out(k)

    def send_out(k):
        @pl.loop(1, NZ)
        def _(d):
            send(
                out_cols.at[k, column_rows(lax.rem(z + d, NZ))], out_rows.at[k, column_rows(z)],
                oz_send.at[k, d], oz_recv.at[k, d], at_z(d),
            )

        out_rows[k, column_rows(z), :] = out_cols[k, column_rows(z), :]

    def out_arrived(k):
        @pl.loop(1, NZ)
        def _(d):
            arrived(out_rows.at[k, column_rows(lax.rem(z + NZ - d, NZ))], oz_recv.at[k, d])

    def turn_out(k):
        out_arrived(k)
        for target in range(NY):
            for token in range(2):
                out_pairs[k, target, token] = out_rows[k, pl.ds(2 * target + token, NZ, stride=8), :]
        for d in (2, 1, 3):
            pending.append(
                send(
                    out_pairs.at[k, lax.rem(y + d, NY)], out_ref.at[k, y],
                    oy_send.at[k, d], oy_recv.at[k, d], at_y(d),
                )
            )
        out_ref[k, y] = out_pairs[k, y]

    def out_here(k):
        for d in (1, 2, 3):
            arrived(out_ref.at[k, lax.rem(y + NY - d, NY)], oy_recv.at[k, d])

    def out_sent(k):
        @pl.loop(1, NZ)
        def _(d):
            ref = out_cols.at[k, column_rows(lax.rem(z + d, NZ))]
            pltpu.make_async_copy(ref, ref, oz_send.at[k, d]).wait()

    start_columns(0)
    start_columns(1)
    matrix_of_rows()
    weights_here(0, wq_all)
    start_sums(0, wq_all, True)
    keeps[2].wait()
    keeps[3].wait()
    lat_gathers[0].finish()
    make_kv(0)
    query_sums = sums(0, True)
    swap_part(2, 512, QUARTER - 512)
    blocks[0, z] = attend(0, query_sums)
    gathers[1].pass_on(0)

    @pl.when(s < 7)
    def _():
        send(lat_all.at[0], lat_all.at[1], lr_send.at[0], lr_recv.at[0], following)

    @pl.when(s == 0)
    def _():
        lat_gathers[1].pass_on(0)

    gathers[1].pass_on(2, 6)
    columns_here(0)
    columns_here(1)
    gathers[1].finish()

    @pl.when(s == 0)
    def _():
        lat_gathers[1].pass_on(2, 6)

    matrix_plain(1)
    keeps[1].wait()
    part_here(1, 0, 512)
    part_here(2, 512, QUARTER - 512)
    start_sums(1, wo_all, False)
    pl.semaphore_wait(k_sem, 1)

    @pl.when(s == 0)
    def _():
        lat_gathers[1].finish()

    made = block_out(sums(1, False), columns[0])
    relay_out[...] = made

    hops = [reached for reached, via in TREE if via == 0]

    @pl.when(s < 7)
    def _():
        for hop in hops:
            send(
                relay_out, blocks.at[1, z], z_send.at[2, hop % NZ], z_recv.at[2, hop % NZ],
                (s + 1, y * NZ + lax.rem(z + hop + NZ, NZ)),
            )
        send(relay_out, blocks.at[1, z], n_send.at[0], n_recv.at[0], following)

    @pl.when(s == 0)
    def _():
        blocks[1, z] = columns[1].astype(jnp.bfloat16)
        for hop in hops:
            send(
                blocks.at[1, z], blocks.at[1, z], z_send.at[3, hop % NZ], z_recv.at[2, hop % NZ],
                at_z(hop),
            )

    start_out(0, made)

    @pl.when(s == 0)
    def _():
        swap_lat(1)

    gathers[2].pass_on(2, 6)

    @pl.when(s > 0)
    def _():
        arrived(blocks.at[1, z], n_recv.at[0])

    gathers[2].finish()
    matrix_of_blocks(2)
    start_sums(2, wq_all, True)

    turn_out(0)

    @pl.when(s == 0)
    def _():
        lat_swapped(1)

    @pl.when(s > 0)
    def _():
        arrived(lat_all.at[1], lr_recv.at[0])

    make_kv(1)
    blocks[2, z] = attend(1, sums(2, True))

    @pl.when(s == 0)
    def _():
        for hop in hops:
            arrived(blocks.at[1, z], z_send.at[3, hop % NZ])

    gathers[3].pass_on(0)
    gathers[3].pass_on(2, 6)
    out_here(0)

    @pl.when(s < 7)
    def _():
        send(out_ref.at[0], entered, h_send.at[0], h_recv.at[0], following)

    gathers[3].finish()
    matrix_plain(3)
    for part in range(NY):
        partial[3, part, pl.ds(0, MB), :] = jnp.dot(
            matrix[...], wo_all[part], preferred_element_type=jnp.float32
        )
        for owner in range(NY):
            for token in range(2):
                split_out[owner, pl.ds(part * 32 + token * NZ, NZ), :] = partial[
                    3, part, pl.ds(2 * owner + token, NZ, stride=8), :
                ]
    for d in (2, 1, 3):
        pending.append(
            send(
                split_out.at[lax.rem(y + d, NY)], others.at[3, y, pl.ds(0, MB)],
                r_send.at[3, d], r_recv.at[3, d], at_y(d),
            )
        )
    for d in (1, 2, 3):
        arrived(gates.at[lax.rem(y + NY - d, NY)], g_recv.at[d])
        arrived(others.at[3, lax.rem(y + NY - d, NY), pl.ds(0, MB)], r_recv.at[3, d])
    total = split_out[y]
    for d in (1, 2, 3):
        total = total + others[3, lax.rem(y + NY - d, NY), pl.ds(0, MB), :]
    for part in range(NY):
        rows = slice(part * 32, part * 32 + 32)
        split_in[rows, :] = (total[rows] * gates[part, 0:1, :]).astype(jnp.bfloat16).astype(jnp.float32)
    for owner in range(NZ):
        out_cols[1, pl.ds(owner * 8, 8), :] = split_in[pl.ds(owner, 8, stride=NZ), :]
    send_out(1)

    @pl.when(s > 0)
    def _():
        arrived(entered, h_recv.at[0])

    @pl.when(s == 0)
    def _():
        for part in range(NY):
            for token in range(2):
                for at in range(NZ):
                    lane = (part * NZ + at) * 128
                    entered[part, token, pl.ds(at, 1), :] = rows32[1, pl.ds(token, 1), pl.ds(lane, 128)]

    out_arrived(1)
    for part in range(NY):
        for token in range(2):
            branch = out_rows[1, pl.ds(2 * part + token, NZ, stride=8), :]
            out_ref[1, part, token] = entered[part, token] + branch

    gathers[0].drain()
    gathers[1].drain()
    gathers[2].drain(False)
    gathers[3].drain()
    lat_gathers[0].drain()
    lat_swap_sent(0)

    @pl.when(s == 0)
    def _():
        lat_swap_sent(1)
        lat_gathers[1].drain()

    @pl.when(s < 7)
    def _():
        for hop in hops:
            arrived(relay_out, z_send.at[2, hop % NZ])
        arrived(relay_out, n_send.at[0])
        arrived(out_ref.at[0], h_send.at[0])
        arrived(lat_all.at[0], lr_send.at[0])

    for copy in pending:
        copy.wait_send()
    for k in range(2):
        columns_sent(k)
        out_sent(k)


def local(section_in, fresh, latents, image_order, token_mask, norm_gain, wq, wkv, wo, alpha):
    vmem = pl.BlockSpec(memory_space=pltpu.VMEM)
    smem = pl.BlockSpec(memory_space=pltpu.SMEM)
    hbm = pl.BlockSpec(memory_space=pl.ANY)
    bf16, f32 = jnp.bfloat16, jnp.float32
    dma = pltpu.SemaphoreType.DMA
    out = pl.pallas_call(
        kernel,
        out_shape=jax.ShapeDtypeStruct((2, NY, 2, NZ, 128), f32),
        in_specs=[vmem, vmem, vmem, smem, vmem, vmem, hbm, hbm, hbm, vmem],
        out_specs=vmem,
        scratch_shapes=[
            pltpu.VMEM((NY, QUARTER, HD), bf16),
            pltpu.VMEM((NY, QUARTER, HD), bf16),
            pltpu.VMEM((VD, 2 * HD), bf16),
            pltpu.VMEM((2, 2, D), f32),
            pltpu.VMEM((2, NY, 2, QUARTER), f32),
            pltpu.VMEM((2, 8, QUARTER), f32),
            pltpu.VMEM((2, MB, 128), f32),
            pltpu.VMEM((NZ, 16, 1024), bf16),
            pltpu.VMEM((3, NZ, MB, 128), bf16),
            pltpu.VMEM((2, NZ, NY, 16, HALF_VD), bf16),
            pltpu.VMEM((2, MB, 128), f32),
            pltpu.VMEM((1, D), f32),
            pltpu.VMEM((MB, QUARTER), bf16),
            pltpu.VMEM((MB, 128), f32),
            pltpu.VMEM((4, NY, MB + 8, 128), f32),
            pltpu.VMEM((4, NY, MB + 8, 128), f32),
            pltpu.VMEM((LAT * IMG, 2 * HD), bf16),
            pltpu.VMEM((MB, 128), bf16),
            pltpu.VMEM((2, MB, 128), f32),
            pltpu.VMEM((2, MB, 128), f32),
            pltpu.VMEM((2, NY, 2, NZ, 128), f32),
            pltpu.VMEM((NY, 8, 128), f32),
            pltpu.VMEM((NY, MB, 128), f32),
            pltpu.VMEM((MB, 128), f32),
            pltpu.VMEM((NY, 2, NZ, 128), f32),
            dma((4,)),
            dma((2, 4)), dma((2, 4)),
            dma((3, 4)), dma((3, 4)),
            dma((4, NZ)), dma((4, NZ)),
            dma((2, NZ)), dma((2, NZ)),
            dma((2, 4)), dma((2, 4)),
            dma((1,)), dma((1,)),
            dma((2, NZ)), dma((2, NZ)),
            dma((4, 4)), dma((4, 4)),
            dma((1,)), dma((1,)),
            pltpu.SemaphoreType.REGULAR,
            dma((2, NZ)), dma((2, NZ)),
            dma((2, 4)), dma((2, 4)),
            dma((4,)), dma((4,)),
            dma((1,)), dma((1,)),
        ],
        compiler_params=pltpu.CompilerParams(
            collective_id=0, has_side_effects=True, vmem_limit_bytes=62 * 2**20
        ),
    )(
        section_in[0], fresh, latents.reshape(72, VD), image_order, token_mask.transpose(0, 2, 1), norm_gain,
        wq[0], wkv[0], wo[0], alpha,
    )
    out = out.transpose(0, 2, 1, 3, 4).reshape(2, 1, 2, D).astype(bf16)
    return out[0], out[1]


def solution(mesh):
    in_specs = (
        P("section", "mp", None),
        P("mp", None),
        P(None, "mp", None),
        P(),
        P(),
        P("section", None),
        P("section", None, "mp"),
        P("section", None, None, "mp"),
        P("section", None, "mp"),
        P("section", "mp"),
    )
    out_specs = (P("section", "mp", None), P("section", "mp", None))
    return jax.shard_map(local, mesh=mesh, in_specs=in_specs, out_specs=out_specs, check_vma=False)
```

```python
import functools

import jax
import jax.numpy as jnp
from jax import lax
from jax.experimental import pallas as pl
from jax.experimental.pallas import tpu as pltpu
from jax.sharding import PartitionSpec as P

MESH = pl.DeviceIdType.MESH

HD = 128
LAT = 64
IMG = 8
MB = 128
D = 8192
VD = 1280
NY = 4
NZ = 16
QUARTER = D // NY
HALF_VD = VD // 2

epsilon = 1e-05
negative_big = -1e30


def both_ways(edges):
    listed = []
    for reached, via in edges:
        listed.append((reached, via))
        if reached != NZ // 2:
            listed.append((-reached, -via))
    return listed


TREE = both_ways([(6, 0), (2, 0), (1, 0), (3, 2), (4, 2), (8, 6), (7, 6), (5, 6)])
LEAN = both_ways([(3, 0), (1, 0), (6, 3), (4, 3), (2, 3), (7, 6), (5, 6), (8, 6)])
STEPS = sorted({reached - via for tree in (TREE, LEAN) for reached, via in tree})


def arrived(ref, sem):
    pltpu.make_async_copy(ref, ref, sem).wait()


class Gather:
    def __init__(self, place, block, send, recv, tree):
        self.place, self.block, self.send, self.recv, self.tree = place, block, send, recv, tree
        self.here = {0}

    def origin(self, offset):
        return self.block(lax.rem(self.place[2] - offset + NZ, NZ))

    def need(self, offset):
        if offset not in self.here:
            self.here.add(offset)
            arrived(self.origin(offset), self.recv(offset % NZ))

    def pass_on(self, *vias):
        s, y, z = self.place
        for reached, via in self.tree:
            if abs(via) in vias:
                self.need(via)
                pltpu.make_async_remote_copy(
                    src_ref=self.origin(via),
                    dst_ref=self.origin(via),
                    send_sem=self.send(reached % NZ),
                    recv_sem=self.recv(reached % NZ),
                    device_id=(s, y * NZ + lax.rem(z + reached - via + NZ, NZ)),
                    device_id_type=MESH,
                ).start()

    def finish(self):
        for reached, _ in self.tree:
            self.need(reached)

    def drain(self, first=True):
        for reached, via in self.tree:
            if via or first:
                arrived(self.origin(via), self.send(reached % NZ))


def kernel(
    section_ref, fresh_ref, latents_ref, order_ref, mask_ref, gain_ref, wq_ref, wkv_ref, wo_ref, alpha_ref,
    out_ref,
    wq_all, wo_all, wkv_all, rows32, entry, stripes, columns, first_blocks, blocks, lat_all, seen_all, gain32,
    matrix, squares, partial, others, kv, relay_out, out_cols, out_rows, out_pairs, gates, split_out, split_in, entered,
    local_sem, y_send, y_recv, w_send, w_recv, z_send, z_recv, l_send, l_recv, ly_send, ly_recv, lr_send, lr_recv,
    c_send, c_recv, r_send, r_recv, n_send, n_recv, k_sem, oz_send, oz_recv, oy_send, oy_recv, g_send, g_recv, h_send, h_recv,
):
    s = lax.axis_index("section")
    mp = lax.axis_index("mp")
    y, z = mp // NZ, lax.rem(mp, NZ)
    place = (s, y, z)

    def at_y(d):
        return (s, lax.rem(y + d, NY) * NZ + z)

    def at_z(d):
        return (s, y * NZ + lax.rem(z + d + NZ, NZ))

    following = (lax.rem(s + 1, 8), mp)
    previous = (lax.rem(s + 7, 8), mp)

    def send(src, dst, send_sem, recv_sem, device):
        copy = pltpu.make_async_remote_copy(
            src_ref=src, dst_ref=dst, send_sem=send_sem, recv_sem=recv_sem,
            device_id=device, device_id_type=MESH,
        )
        copy.start()
        return copy

    pending = []

    def signal(sem, device):
        pl.semaphore_signal(sem, inc=1, device_id=device, device_id_type=MESH)

    def quarter(ref, which):
        return ref.at[pl.ds(pl.multiple_of(which * QUARTER, QUARTER), QUARTER)]

    keeps = [
        pltpu.make_async_copy(quarter(wq_ref, y), wq_all.at[y], local_sem.at[0]),
        pltpu.make_async_copy(quarter(wo_ref, y), wo_all.at[y], local_sem.at[1]),
        pltpu.make_async_copy(wkv_ref.at[0], wkv_all.at[:, pl.ds(0, HD)], local_sem.at[2]),
        pltpu.make_async_copy(wkv_ref.at[1], wkv_all.at[:, pl.ds(HD, HD)], local_sem.at[3]),
    ]
    for copy in keeps:
        copy.start()

    barrier = pltpu.get_barrier_semaphore()
    greeted = [at_z(d) for d in STEPS] + [at_y(d) for d in (1, 2, 3)] + [following, previous]
    for device in greeted:
        signal(barrier, device)

    rows32[0] = section_ref[...].astype(jnp.float32)
    rows32[1] = fresh_ref[...].astype(jnp.float32)
    image_row = lax.broadcasted_iota(jnp.int32, (2 * IMG, 72), 0)
    image_lane = lax.broadcasted_iota(jnp.int32, (2 * IMG, 72), 1)
    chosen = jnp.zeros((2 * IMG, 72), jnp.float32)
    for i in range(2 * IMG):
        image = order_ref[(7 - s) * IMG + i]
        chosen = jnp.where((image_row == i) & (image_lane == image), 1.0, chosen)
    picked = jnp.dot(
        chosen.astype(jnp.bfloat16), latents_ref[...], preferred_element_type=jnp.float32
    )

    def keep_lat(k):
        rows = picked[k * IMG:k * IMG + IMG]
        lat_all[k, z, y] = jnp.concatenate([rows[:, :HALF_VD], rows[:, HALF_VD:]], axis=0).astype(jnp.bfloat16)

    keep_lat(0)

    @pl.when(s == 0)
    def _():
        keep_lat(1)

    pl.semaphore_wait(barrier, len(greeted))

    def swap_rows(k):
        for d in (2, 1, 3):
            target = lax.rem(y + d, NY)
            pending.append(
                send(
                    rows32.at[k, :, pl.ds(pl.multiple_of(target * QUARTER, QUARTER), QUARTER)], entry.at[k, y],
                    y_send.at[k, d], y_recv.at[k, d], at_y(d),
                )
            )

    def rows_here(k):
        entry[k, y] = rows32[k, :, pl.ds(pl.multiple_of(y * QUARTER, QUARTER), QUARTER)]
        for d in (1, 2, 3):
            arrived(entry.at[k, lax.rem(y + NY - d, NY)], y_recv.at[k, d])
        for at in range(NY):
            stripes[k, pl.ds(2 * at, 2), :] = entry[k, at]

    def swap_weights(k, src, dst):
        for d in (2, 1, 3):
            pending.append(
                send(
                    quarter(src, lax.rem(y + d, NY)), dst.at[y],
                    w_send.at[k, d], w_recv.at[k, d], at_y(d),
                )
            )

    def swap_part(k, start, count):
        for d in (2, 1, 3):
            pending.append(
                send(
                    wo_ref.at[pl.ds(pl.multiple_of(lax.rem(y + d, NY) * QUARTER + start, 16), count)],
                    wo_all.at[y, pl.ds(start, count)],
                    w_send.at[k, d], w_recv.at[k, d], at_y(d),
                )
            )

    def part_here(k, start, count):
        for d in (1, 2, 3):
            arrived(wo_all.at[lax.rem(y + NY - d, NY), pl.ds(start, count)], w_recv.at[k, d])

    def weights_here(k, dst):
        keeps[k].wait()
        for d in (1, 2, 3):
            arrived(dst.at[lax.rem(y + NY - d, NY)], w_recv.at[k, d])

    lat_gathers = [
        Gather(
            place, (lambda at: lat_all.at[1, at, y]) if k else (lambda at: lat_all.at[0, at]),
            lambda i, k=k: l_send.at[k, i], lambda i, k=k: l_recv.at[k, i], TREE if k else LEAN,
        )
        for k in range(2)
    ]

    def lat_part(k, which):
        return lat_all.at[k, :, which] if k else lat_all.at[k, z, which]

    def swap_lat(k):
        for d in (2, 1, 3):
            send(lat_part(k, y), lat_part(k, y), ly_send.at[k, d], ly_recv.at[k, d], at_y(d))

    def lat_swapped(k):
        for d in (1, 2, 3):
            arrived(lat_part(k, lax.rem(y + NY - d, NY)), ly_recv.at[k, d])

    def lat_swap_sent(k):
        for d in (1, 2, 3):
            arrived(lat_part(k, y), ly_send.at[k, d])

    gates[y] = jnp.broadcast_to(jnp.tanh(alpha_ref[...]), (8, 128))
    swap_rows(0)
    swap_lat(0)
    for d in (2, 1, 3):
        pending.append(send(gates.at[y], gates.at[y], g_send.at[d], g_recv.at[d], at_y(d)))
    swap_rows(1)
    swap_weights(0, wq_ref, wq_all)
    swap_part(1, 0, 1024)
    gain32[...] = gain_ref[...].astype(jnp.float32)

    row_at = lax.broadcasted_iota(jnp.int32, (MB, MB), 0)
    lane_at = lax.broadcasted_iota(jnp.int32, (MB, MB), 1)
    token = ((row_at >> 1) & 3) * 32 + (row_at >> 3) * 2 + (row_at & 1)
    reorder = jnp.where(lane_at == token, 1.0, 0.0).astype(jnp.bfloat16)
    slot_at = lax.broadcasted_iota(jnp.int32, (IMG, MB), 0)
    slot_lane = lax.broadcasted_iota(jnp.int32, (IMG, MB), 1)
    repeat = jnp.where((slot_lane & 7) == slot_at, 1.0, 0.0).astype(jnp.bfloat16)
    for k in range(2):
        slots = mask_ref[7 - s + k].astype(jnp.float32).astype(jnp.bfloat16)
        slots = lax.dot_general(
            reorder, slots, (((1,), (1,)), ((), ())), preferred_element_type=jnp.float32
        )
        seen_all[k] = jnp.dot(slots.astype(jnp.bfloat16), repeat, preferred_element_type=jnp.float32)

    def make_kv(k):
        @pl.loop(0, 4)
        def _(part):
            held = lat_all[k, pl.ds(part * 4, 4)].reshape(NZ * 16, HALF_VD)
            low = jnp.dot(held, wkv_all[:HALF_VD, :], preferred_element_type=jnp.float32)
            high = jnp.dot(held, wkv_all[HALF_VD:, :], preferred_element_type=jnp.float32)
            low = low.reshape(NZ, 16, 2 * HD)[:, :8]
            high = high.reshape(NZ, 16, 2 * HD)[:, 8:]
            made = (low + high).reshape(NZ * IMG, 2 * HD).astype(jnp.bfloat16)
            kv[pl.ds(pl.multiple_of(part * 128, 128), 128), :] = made

    gathers = [
        Gather(
            place,
            (lambda at: first_blocks.at[at]) if g == 0 else (lambda at, g=g: blocks.at[g - 1, at]),
            lambda i, g=g: z_send.at[g, i], lambda i, g=g: z_recv.at[g, i], TREE,
        )
        for g in range(4)
    ]

    rows_here(0)
    first_blocks[z] = jnp.concatenate(
        [stripes[0, :, pl.ds(0, 1024)], stripes[0, :, pl.ds(1024, 1024)]], axis=0
    ).astype(jnp.bfloat16)
    gathers[0].pass_on(0)
    lat_swapped(0)
    lat_gathers[0].pass_on(0)
    gathers[0].pass_on(2, 6)
    lat_gathers[0].pass_on(3)
    rows_here(1)
    gathers[0].finish()
    signal(k_sem, previous)
    lat_gathers[0].pass_on(6)

    def column_rows(which):
        return pl.ds(pl.multiple_of(which * 8, 8), 8)

    def lanes(which):
        return pl.ds(pl.multiple_of(which * 128, 128), 128)

    def start_columns(k):
        @pl.loop(1, NZ)
        def _(d):
            target = lax.rem(z + d, NZ)
            send(
                stripes.at[k, :, lanes(target)], columns.at[k, column_rows(z)],
                c_send.at[k, d], c_recv.at[k, d], at_z(d),
            )

        columns[k, column_rows(z), :] = stripes[k, :, lanes(z)]

    def columns_here(k):
        @pl.loop(1, NZ)
        def _(d):
            arrived(columns.at[k, column_rows(lax.rem(z + NZ - d, NZ))], c_recv.at[k, d])

    def columns_sent(k):
        @pl.loop(1, NZ)
        def _(d):
            ref = stripes.at[k, :, lanes(lax.rem(z + d, NZ))]
            pltpu.make_async_copy(ref, ref, c_send.at[k, d]).wait()

    gain_here = gain32[:, pl.ds(pl.multiple_of(y * QUARTER, QUARTER), QUARTER)]

    def matrix_of_rows():
        @pl.loop(0, NZ // 2)
        def _(pair):
            one = first_blocks[2 * pair].astype(jnp.float32)
            two = first_blocks[2 * pair + 1].astype(jnp.float32)
            total = jnp.zeros((16, 128), jnp.float32)
            where = pl.ds(pl.multiple_of(pair * 16, 16), 16)
            for half in range(2):
                part = jnp.concatenate([one[half * 8:half * 8 + 8], two[half * 8:half * 8 + 8]], axis=0)
                for lane in range(8):
                    cut = part[:, lane * 128:lane * 128 + 128]
                    total = total + cut * cut
                gain_part = gain_here[:, half * 1024:half * 1024 + 1024]
                matrix[where, pl.ds(half * 1024, 1024)] = (part * gain_part).astype(jnp.bfloat16)
            squares[where, :] = total

    def matrix_of_blocks(g):
        squares[...] = jnp.zeros_like(squares)
        for at in range(NZ):
            block = blocks[g - 1, at].astype(jnp.float32)
            squares[...] += block * block
            matrix[:, pl.ds(at * 128, 128)] = (
                block * gain_here[:, at * 128:at * 128 + 128]
            ).astype(jnp.bfloat16)

    def matrix_plain(g):
        for at in range(NZ):
            matrix[:, pl.ds(at * 128, 128)] = blocks[g - 1, at]

    def start_sums(g, weights, with_squares):
        rows = MB + 8 if with_squares else MB
        if with_squares:
            row = jnp.sum(squares[...].T, axis=0, keepdims=True)
            row = jnp.broadcast_to(row, (8, 128))
        for d in (2, 1, 3, 0):
            target = lax.rem(y + d, NY)
            partial[g, target, pl.ds(0, MB), :] = jnp.dot(
                matrix[...], weights[target], preferred_element_type=jnp.float32
            )
            if with_squares:
                partial[g, target, pl.ds(MB, 8), :] = row
            if d:
                pending.append(
                    send(
                        partial.at[g, target, pl.ds(0, rows)], others.at[g, y, pl.ds(0, rows)],
                        r_send.at[g, d], r_recv.at[g, d], at_y(d),
                    )
                )

    def sums(g, with_squares):
        rows = MB + 8 if with_squares else MB
        for d in (1, 2, 3):
            arrived(others.at[g, lax.rem(y + NY - d, NY), pl.ds(0, rows)], r_recv.at[g, d])
        total = partial[g, y, pl.ds(0, rows), :]
        for d in (1, 2, 3):
            total = total + others[g, lax.rem(y + NY - d, NY), pl.ds(0, rows), :]
        return total

    def attend(k, total):
        row = jnp.broadcast_to(total[MB:MB + 1, :], (128, 128))
        scale = lax.rsqrt(row.T * (1.0 / D) + epsilon)
        queries = (total[:MB] * scale).astype(jnp.bfloat16)
        scores = lax.dot_general(
            queries, kv[:, :HD], (((1,), (1,)), ((), ())), preferred_element_type=jnp.float32
        ) * HD ** (-0.5)
        seen = seen_all[k]
        visible = jnp.concatenate([seen] * 4, axis=1) > 0
        seen_any = jnp.max(seen, axis=1, keepdims=True) > 0
        largest = jnp.max(jnp.where(visible, scores, negative_big), axis=1, keepdims=True)
        largest = jnp.where(seen_any, largest, 0.0)
        expanded = jnp.where(visible, jnp.exp(jnp.where(visible, scores - largest, 0.0)), 0.0)
        totals = jnp.sum(expanded, axis=1, keepdims=True)
        totals = jnp.where(seen_any, totals, 1.0)
        probs = (expanded / totals).astype(jnp.bfloat16)
        return jnp.dot(probs, kv[:, HD:], preferred_element_type=jnp.float32).astype(jnp.bfloat16)

    gate = jnp.tanh(alpha_ref[...])

    def block_out(total, hidden):
        branch = (total * gate).astype(jnp.bfloat16).astype(jnp.float32)
        return (hidden + branch).astype(jnp.bfloat16)

    def start_out(k, made):
        out_cols[k] = made.astype(jnp.float32)
        send_out(k)

    def send_out(k):
        @pl.loop(1, NZ)
        def _(d):
            send(
                out_cols.at[k, column_rows(lax.rem(z + d, NZ))], out_rows.at[k, column_rows(z)],
                oz_send.at[k, d], oz_recv.at[k, d], at_z(d),
            )

        out_rows[k, column_rows(z), :] = out_cols[k, column_rows(z), :]

    def out_arrived(k):
        @pl.loop(1, NZ)
        def _(d):
            arrived(out_rows.at[k, column_rows(lax.rem(z + NZ - d, NZ))], oz_recv.at[k, d])

    def turn_out(k):
        out_arrived(k)
        for target in range(NY):
            for token in range(2):
                out_pairs[k, target, token] = out_rows[k, pl.ds(2 * target + token, NZ, stride=8), :]
        for d in (2, 1, 3):
            pending.append(
                send(
                    out_pairs.at[k, lax.rem(y + d, NY)], out_ref.at[k, y],
                    oy_send.at[k, d], oy_recv.at[k, d], at_y(d),
                )
            )
        out_ref[k, y] = out_pairs[k, y]

    def out_here(k):
        for d in (1, 2, 3):
            arrived(out_ref.at[k, lax.rem(y + NY - d, NY)], oy_recv.at[k, d])

    def out_sent(k):
        @pl.loop(1, NZ)
        def _(d):
            ref = out_cols.at[k, column_rows(lax.rem(z + d, NZ))]
            pltpu.make_async_copy(ref, ref, oz_send.at[k, d]).wait()

    start_columns(0)
    start_columns(1)
    matrix_of_rows()
    weights_here(0, wq_all)
    start_sums(0, wq_all, True)
    keeps[2].wait()
    keeps[3].wait()
    lat_gathers[0].finish()
    make_kv(0)
    query_sums = sums(0, True)
    swap_part(2, 1024, QUARTER - 1024)
    blocks[0, z] = attend(0, query_sums)
    gathers[1].pass_on(0)

    @pl.when(s < 7)
    def _():
        send(lat_all.at[0], lat_all.at[1], lr_send.at[0], lr_recv.at[0], following)

    @pl.when(s == 0)
    def _():
        lat_gathers[1].pass_on(0)

    gathers[1].pass_on(2, 6)
    columns_here(0)
    columns_here(1)
    gathers[1].finish()

    @pl.when(s == 0)
    def _():
        lat_gathers[1].pass_on(2, 6)

    matrix_plain(1)
    keeps[1].wait()
    part_here(1, 0, 1024)
    part_here(2, 1024, QUARTER - 1024)
    start_sums(1, wo_all, False)
    pl.semaphore_wait(k_sem, 1)

    @pl.when(s == 0)
    def _():
        lat_gathers[1].finish()

    made = block_out(sums(1, False), columns[0])
    relay_out[...] = made

    hops = [reached for reached, via in TREE if via == 0]

    @pl.when(s < 7)
    def _():
        for hop in hops:
            send(
                relay_out, blocks.at[1, z], z_send.at[2, hop % NZ], z_recv.at[2, hop % NZ],
                (s + 1, y * NZ + lax.rem(z + hop + NZ, NZ)),
            )
        send(relay_out, blocks.at[1, z], n_send.at[0], n_recv.at[0], following)

    @pl.when(s == 0)
    def _():
        blocks[1, z] = columns[1].astype(jnp.bfloat16)
        for hop in hops:
            send(
                blocks.at[1, z], blocks.at[1, z], z_send.at[3, hop % NZ], z_recv.at[2, hop % NZ],
                at_z(hop),
            )

    start_out(0, made)

    @pl.when(s == 0)
    def _():
        swap_lat(1)

    gathers[2].pass_on(2, 6)

    @pl.when(s > 0)
    def _():
        arrived(blocks.at[1, z], n_recv.at[0])

    gathers[2].finish()
    matrix_of_blocks(2)
    start_sums(2, wq_all, True)

    turn_out(0)

    @pl.when(s == 0)
    def _():
        lat_swapped(1)

    @pl.when(s > 0)
    def _():
        arrived(lat_all.at[1], lr_recv.at[0])

    make_kv(1)
    blocks[2, z] = attend(1, sums(2, True))

    @pl.when(s == 0)
    def _():
        for hop in hops:
            arrived(blocks.at[1, z], z_send.at[3, hop % NZ])

    gathers[3].pass_on(0)
    gathers[3].pass_on(2, 6)
    out_here(0)

    @pl.when(s < 7)
    def _():
        send(out_ref.at[0], entered, h_send.at[0], h_recv.at[0], following)

    gathers[3].finish()
    matrix_plain(3)
    for part in range(NY):
        partial[3, part, pl.ds(0, MB), :] = jnp.dot(
            matrix[...], wo_all[part], preferred_element_type=jnp.float32
        )
        for owner in range(NY):
            for token in range(2):
                split_out[owner, pl.ds(part * 32 + token * NZ, NZ), :] = partial[
                    3, part, pl.ds(2 * owner + token, NZ, stride=8), :
                ]
    for d in (2, 1, 3):
        pending.append(
            send(
                split_out.at[lax.rem(y + d, NY)], others.at[3, y, pl.ds(0, MB)],
                r_send.at[3, d], r_recv.at[3, d], at_y(d),
            )
        )
    for d in (1, 2, 3):
        arrived(gates.at[lax.rem(y + NY - d, NY)], g_recv.at[d])
        arrived(others.at[3, lax.rem(y + NY - d, NY), pl.ds(0, MB)], r_recv.at[3, d])
    total = split_out[y]
    for d in (1, 2, 3):
        total = total + others[3, lax.rem(y + NY - d, NY), pl.ds(0, MB), :]
    for part in range(NY):
        rows = slice(part * 32, part * 32 + 32)
        split_in[rows, :] = (total[rows] * gates[part, 0:1, :]).astype(jnp.bfloat16).astype(jnp.float32)
    for owner in range(NZ):
        out_cols[1, pl.ds(owner * 8, 8), :] = split_in[pl.ds(owner, 8, stride=NZ), :]
    send_out(1)

    @pl.when(s > 0)
    def _():
        arrived(entered, h_recv.at[0])

    @pl.when(s == 0)
    def _():
        for part in range(NY):
            for token in range(2):
                for at in range(NZ):
                    lane = (part * NZ + at) * 128
                    entered[part, token, pl.ds(at, 1), :] = rows32[1, pl.ds(token, 1), pl.ds(lane, 128)]

    out_arrived(1)
    for part in range(NY):
        for token in range(2):
            branch = out_rows[1, pl.ds(2 * part + token, NZ, stride=8), :]
            out_ref[1, part, token] = entered[part, token] + branch

    gathers[0].drain()
    gathers[1].drain()
    gathers[2].drain(False)
    gathers[3].drain()
    lat_gathers[0].drain()
    lat_swap_sent(0)

    @pl.when(s == 0)
    def _():
        lat_swap_sent(1)
        lat_gathers[1].drain()

    @pl.when(s < 7)
    def _():
        for hop in hops:
            arrived(relay_out, z_send.at[2, hop % NZ])
        arrived(relay_out, n_send.at[0])
        arrived(out_ref.at[0], h_send.at[0])
        arrived(lat_all.at[0], lr_send.at[0])

    for copy in pending:
        copy.wait_send()
    for k in range(2):
        columns_sent(k)
        out_sent(k)


def local(section_in, fresh, latents, image_order, token_mask, norm_gain, wq, wkv, wo, alpha):
    vmem = pl.BlockSpec(memory_space=pltpu.VMEM)
    smem = pl.BlockSpec(memory_space=pltpu.SMEM)
    hbm = pl.BlockSpec(memory_space=pl.ANY)
    bf16, f32 = jnp.bfloat16, jnp.float32
    dma = pltpu.SemaphoreType.DMA
    out = pl.pallas_call(
        kernel,
        out_shape=jax.ShapeDtypeStruct((2, NY, 2, NZ, 128), f32),
        in_specs=[vmem, vmem, vmem, smem, vmem, vmem, hbm, hbm, hbm, vmem],
        out_specs=vmem,
        scratch_shapes=[
            pltpu.VMEM((NY, QUARTER, HD), bf16),
            pltpu.VMEM((NY, QUARTER, HD), bf16),
            pltpu.VMEM((VD, 2 * HD), bf16),
            pltpu.VMEM((2, 2, D), f32),
            pltpu.VMEM((2, NY, 2, QUARTER), f32),
            pltpu.VMEM((2, 8, QUARTER), f32),
            pltpu.VMEM((2, MB, 128), f32),
            pltpu.VMEM((NZ, 16, 1024), bf16),
            pltpu.VMEM((3, NZ, MB, 128), bf16),
            pltpu.VMEM((2, NZ, NY, 16, HALF_VD), bf16),
            pltpu.VMEM((2, MB, 128), f32),
            pltpu.VMEM((1, D), f32),
            pltpu.VMEM((MB, QUARTER), bf16),
            pltpu.VMEM((MB, 128), f32),
            pltpu.VMEM((4, NY, MB + 8, 128), f32),
            pltpu.VMEM((4, NY, MB + 8, 128), f32),
            pltpu.VMEM((LAT * IMG, 2 * HD), bf16),
            pltpu.VMEM((MB, 128), bf16),
            pltpu.VMEM((2, MB, 128), f32),
            pltpu.VMEM((2, MB, 128), f32),
            pltpu.VMEM((2, NY, 2, NZ, 128), f32),
            pltpu.VMEM((NY, 8, 128), f32),
            pltpu.VMEM((NY, MB, 128), f32),
            pltpu.VMEM((MB, 128), f32),
            pltpu.VMEM((NY, 2, NZ, 128), f32),
            dma((4,)),
            dma((2, 4)), dma((2, 4)),
            dma((3, 4)), dma((3, 4)),
            dma((4, NZ)), dma((4, NZ)),
            dma((2, NZ)), dma((2, NZ)),
            dma((2, 4)), dma((2, 4)),
            dma((1,)), dma((1,)),
            dma((2, NZ)), dma((2, NZ)),
            dma((4, 4)), dma((4, 4)),
            dma((1,)), dma((1,)),
            pltpu.SemaphoreType.REGULAR,
            dma((2, NZ)), dma((2, NZ)),
            dma((2, 4)), dma((2, 4)),
            dma((4,)), dma((4,)),
            dma((1,)), dma((1,)),
        ],
        compiler_params=pltpu.CompilerParams(
            collective_id=0, has_side_effects=True, vmem_limit_bytes=62 * 2**20
        ),
    )(
        section_in[0], fresh, latents.reshape(72, VD), image_order, token_mask.transpose(0, 2, 1), norm_gain,
        wq[0], wkv[0], wo[0], alpha,
    )
    out = out.transpose(0, 2, 1, 3, 4).reshape(2, 1, 2, D).astype(bf16)
    return out[0], out[1]


def solution(mesh):
    in_specs = (
        P("section", "mp", None),
        P("mp", None),
        P(None, "mp", None),
        P(),
        P(),
        P("section", None),
        P("section", None, "mp"),
        P("section", None, None, "mp"),
        P("section", None, "mp"),
        P("section", "mp"),
    )
    out_specs = (P("section", "mp", None), P("section", "mp", None))
    return jax.shard_map(local, mesh=mesh, in_specs=in_specs, out_specs=out_specs, check_vma=False)
```
